32 devices in a mesh: dp: 4 (over x, core), tm: 8 (over z, y).
Axes of the slice: x: 2, y: 2, z: 4, core: 2. Of those that a mesh axis runs over, the one named last changes fastest.
Arguments:
- latents: bfloat16 [4, 17, 16, 64, 256], P('dp', None, 'tm'), may hold values from -6 to 6
- cotangent: bfloat16 [4, 17, 16, 64, 256], P('dp', None, 'tm'), may hold values from -6 to 6
- spatial_weight: bfloat16 [3, 3, 256, 256], replicated, may hold values from -0.125 to 0.125
- temporal_weight: bfloat16 [3, 256, 256], replicated, may hold values from -0.21875 to 0.21875
Outputs:
- block_out: bfloat16 [4, 17, 16, 64, 256], P('dp', None, 'tm')
- latents_grad: bfloat16 [4, 17, 16, 64, 256], P('dp', None, 'tm')
- spatial_grad: float32 [3, 3, 256, 256], replicated
- temporal_grad: float32 [3, 256, 256], replicated
The draws below stay inside these ranges and needn't reach their ends.
All inputs are finite; a program needn't handle non-finite values.
Results may differ from the reference program's by a relative error of at most 0.0085.
Values may be sent and summed in bfloat16 or wider, within the bound.
No kernel may reach another device: no remote copies, remote signals or barrier semaphores. Data moves between devices by JAX's collectives and lax.ppermute only.
A program may use at most 64 MiB of HBM per device.

```python
import jax
import jax.numpy as jnp
from jax import lax

C = 256
FRAMES = 17
W = 64
CLIPS = 4
ROWS = 16


def steps_of(rng, extent, cuts, smallest, high):
    def one(axis_at, blocks):
        heights = jax.random.uniform(jax.random.fold_in(jax.random.fold_in(rng, 6), axis_at), (blocks,), jnp.float32, smallest / len(cuts), high / len(cuts))
        return jnp.repeat(jnp.exp(heights), extent[axis_at] // blocks).reshape((-1,) + (1,) * (len(extent) - axis_at - 1))

    gain = one(*cuts[0])
    for cut in cuts[1:]:
        gain = gain * one(*cut)
    return gain


def normal_values(key, dims, deviation, limit, shards=(), dtype=jnp.bfloat16):
    result = jax.random.normal(key, dims, jnp.float32) * deviation
    if len(shards) > 0:
        result = steps_of(key, dims, shards, -0.22, 0.18) * result
    return jnp.clip(result, min=-limit, max=limit).astype(dtype)


def setup_inputs(seed: int = 0) -> dict:
    key_list = jax.random.split(jax.random.key(seed), 5)
    latents = normal_values(key_list[0], (CLIPS, FRAMES, ROWS, W, C), 1.0, 6.0, ((0, 4), (2, 8)))
    cotangent = normal_values(key_list[1], (CLIPS, FRAMES, ROWS, W, C), 1.0, 6.0, ((0, 4), (2, 8)))
    spatial_weight = normal_values(key_list[2], (3, 3, C, C), (9 * C) ** -0.5, 0.125)
    temporal_weight = normal_values(key_list[3], (3, C, C), (3 * C) ** -0.5, 0.21875)
    return dict(latents=latents, cotangent=cotangent, spatial_weight=spatial_weight, temporal_weight=temporal_weight)


def window_patches(field, flipped):
    padded = jnp.pad(field, ((0, 0), (1, 1), (1, 1), (0, 0)))
    rows = field.shape[1]
    cols = field.shape[2]
    pieces = []
    for first in range(3):
        for second in range(3):
            top = 2 - first if flipped else first
            left = 2 - second if flipped else second
            pieces.append(padded[:, top:top + rows, left:left + cols, :])
    return jnp.concatenate(pieces, axis=3).reshape(-1, 9 * field.shape[3])


def one_clip(inputs):
    latents, cotangent, spatial_weight, temporal_weight = inputs
    frames, rows, cols, chans = latents.shape
    flat_w = spatial_weight.reshape(9 * chans, chans)
    flip_w = jnp.transpose(spatial_weight, (0, 1, 3, 2)).reshape(9 * chans, chans)
    patches = window_patches(latents, False)
    pre = jnp.dot(patches, flat_w, preferred_element_type=jnp.float32)
    act = jax.nn.silu(pre).astype(jnp.bfloat16)
    act3 = act.reshape(frames, rows * cols, chans)
    cot3 = cotangent.reshape(frames, rows * cols, chans)
    act_pad = jnp.pad(act3, ((2, 0), (0, 0), (0, 0)))
    cot_pad = jnp.pad(cot3, ((0, 2), (0, 0), (0, 0)))
    mixed = jnp.zeros((frames * rows * cols, chans), jnp.float32)
    act_grad = jnp.zeros((frames * rows * cols, chans), jnp.float32)
    temporal_parts = []
    cot_flat = cot3.reshape(-1, chans)
    for tap in range(3):
        earlier = act_pad[2 - tap:2 - tap + frames].reshape(-1, chans)
        later = cot_pad[tap:tap + frames].reshape(-1, chans)
        mixed = mixed + jnp.dot(earlier, temporal_weight[tap], preferred_element_type=jnp.float32)
        act_grad = act_grad + jnp.dot(later, temporal_weight[tap].T, preferred_element_type=jnp.float32)
        temporal_parts.append(jnp.dot(earlier.T, cot_flat, preferred_element_type=jnp.float32))
    mixed = mixed.astype(jnp.bfloat16)
    act_grad = act_grad.astype(jnp.bfloat16)
    block_out = (latents.reshape(-1, chans).astype(jnp.float32) + mixed.astype(jnp.float32)).astype(jnp.bfloat16)
    sig = jax.nn.sigmoid(pre)
    pre_grad = (act_grad.astype(jnp.float32) * sig * (1.0 + pre * (1.0 - sig))).astype(jnp.bfloat16)
    back = jnp.dot(window_patches(pre_grad.reshape(frames, rows, cols, chans), True), flip_w, preferred_element_type=jnp.float32)
    latents_grad = (cotangent.reshape(-1, chans).astype(jnp.float32) + back).astype(jnp.bfloat16)
    spatial_part = jnp.dot(patches.T, pre_grad, preferred_element_type=jnp.float32)
    return (block_out.reshape(latents.shape), latents_grad.reshape(latents.shape), spatial_part, jnp.stack(temporal_parts))


def reference(latents, cotangent, spatial_weight, temporal_weight):
    clips, frames, rows, cols, chans = latents.shape
    weights_s = jnp.broadcast_to(spatial_weight, (clips,) + spatial_weight.shape)
    weights_t = jnp.broadcast_to(temporal_weight, (clips,) + temporal_weight.shape)
    block_out, latents_grad, spatial_parts, temporal_parts = lax.map(one_clip, (latents, cotangent, weights_s, weights_t))
    scale = (clips * frames * rows * cols) ** -0.5
    spatial_grad = jnp.sum(spatial_parts, axis=0) * scale
    temporal_grad = jnp.sum(temporal_parts, axis=0) * scale
    return (block_out, latents_grad, spatial_grad.reshape(3, 3, chans, chans), temporal_grad)
```

```python
import functools

import jax
import jax.numpy as jnp
from jax import lax
from jax.experimental import pallas as pl
from jax.experimental.pallas import tpu as pltpu
from jax.sharding import PartitionSpec as P

BF16 = jnp.bfloat16
F32 = jnp.float32
TILE_ROWS = 16
VMEM = pl.BlockSpec(memory_space=pltpu.VMEM)
SMEM = pl.BlockSpec(memory_space=pltpu.SMEM)


def mm(a, b):
    return jnp.dot(a, b, preferred_element_type=F32)


def mm_t(a, b):
    return lax.dot_general(a, b, (((1,), (1,)), ((), ())), preferred_element_type=F32)


def outer(a, b):
    return lax.dot_general(a, b, (((0,), (0,)), ((), ())), preferred_element_type=F32)


def call(kernel, outs, scratch, vmem_mb, flops, *args):
    size = sum(a.size * a.dtype.itemsize for a in args)
    size += sum(o.size * o.dtype.itemsize for o in outs)
    return pl.pallas_call(
        kernel,
        out_shape=outs,
        in_specs=[SMEM if a.dtype == jnp.int32 else VMEM for a in args],
        out_specs=[VMEM] * len(outs),
        scratch_shapes=scratch,
        compiler_params=pltpu.CompilerParams(vmem_limit_bytes=vmem_mb << 20),
        cost_estimate=pl.CostEstimate(flops=flops, bytes_accessed=size, transcendentals=0),
    )(*args)


def shift_right(tile):
    w = lax.broadcasted_iota(jnp.int32, tile.shape, 0)
    return jnp.where(w == 0, 0.0, pltpu.roll(tile, 1, 0))


def shift_left(tile):
    w = lax.broadcasted_iota(jnp.int32, tile.shape, 0)
    last = tile.shape[0] - 1
    return jnp.where(w == last, 0.0, pltpu.roll(tile, last, 0))


def row_of(ref, row):
    frames, _, cols, chans = ref.shape
    return ref[:, row].reshape(frames * cols, chans)


def first_kernel(shift, lat, cot, ws, wt, pre_loc, act_grad, taps, cot_pad):
    frames, rows, cols, chans = lat.shape
    cells = frames * cols
    for row in range(rows):
        for b in range(3):
            total = None
            for a in range(3):
                if 0 <= row + a - 1 < rows:
                    part = mm(row_of(lat, row + a - 1), ws[a, b])
                    total = part if total is None else total + part
            taps[b] = total

        @pl.loop(0, frames)
        def _(f):
            at = pl.ds(pl.multiple_of(f * cols, cols), cols)
            pre_loc[row, at] = shift_right(taps[0, at]) + taps[1, at] + shift_left(taps[2, at])

        cot_pad[:cells] = row_of(cot, row)
        cot_pad[cells:] = jnp.zeros((2 * shift, chans), BF16)
        total = mm_t(cot_pad[:cells], wt[0])
        total += mm_t(cot_pad[pl.ds(shift, cells)], wt[1])
        total += mm_t(cot_pad[pl.ds(2 * shift, cells)], wt[2])
        act_grad[row] = total.astype(BF16)


def grads_kernel(
    shift, slots, scale, code, lat, cot, above, below, pre_loc, act_grad, ws, act, pg, sums, taps, spread, cots, total
):
    frames, rows, cols, chans = lat.shape
    cells = frames * cols
    for row in range(rows):
        halos = []
        if row == 0:
            halos.append((0, above))
        if row == rows - 1:
            halos.append((2, below))
        for b in range(3):
            for n, (a, halo) in enumerate(halos):
                part = mm(halo[...], ws[a, b])
                taps[b] = part if n == 0 else taps[b] + part

        @pl.loop(0, frames)
        def _(f):
            at = pl.ds(pl.multiple_of(f * cols, cols), cols)
            pre = pre_loc[row, at]
            if halos:
                pre += shift_right(taps[0, at]) + taps[1, at] + shift_left(taps[2, at])
            sig = 1.0 / (1.0 + jnp.exp(-pre))
            act[row, at] = (pre * sig).astype(BF16)
            grad = act_grad[row, at].astype(F32) * sig * (1.0 + pre * (1.0 - sig))
            grad16 = grad.astype(BF16)
            pg[row, at] = grad16
            grad = grad16.astype(F32)
            spread[at, :chans] = shift_left(grad).astype(BF16)
            spread[at, chans : 2 * chans] = grad16
            spread[at, 2 * chans :] = shift_right(grad).astype(BF16)

        cot_row = row_of(cot, row)
        for k in range(3):
            cots[: cells - k * shift, k * chans : (k + 1) * chans] = cot_row[k * shift :]
            if k:
                cots[cells - k * shift :, k * chans : (k + 1) * chans] = jnp.zeros((k * shift, chans), BF16)
        for a in range(3):
            at = row + a - 1
            cells_in = above[...] if at < 0 else below[...] if at == rows else row_of(lat, at)
            part = outer(cells_in, spread[...])
            total[a * chans : (a + 1) * chans] = part if row == 0 else total[a * chans : (a + 1) * chans] + part
        part = outer(act[row], cots[...])
        total[3 * chans :] = part if row == 0 else total[3 * chans :] + part
    size = total.shape[0] // slots
    for slot in range(slots):
        at = pl.multiple_of((slot ^ code[0]) * size, size)
        sums[slot * size : (slot + 1) * size] = (total[pl.ds(at, size)] * scale).astype(BF16)


def out_kernel(shift, lat, cot, act, pg, ws, wt, block_out, back_loc, taps, act_pad):
    frames, rows, cols, chans = lat.shape
    cells = frames * cols
    for row in range(rows):
        act_pad[: 2 * shift] = jnp.zeros((2 * shift, chans), BF16)
        act_pad[2 * shift :] = act[row]
        mixed = mm(act_pad[pl.ds(2 * shift, cells)], wt[0])
        mixed += mm(act_pad[pl.ds(shift, cells)], wt[1])
        mixed += mm(act_pad[:cells], wt[2])
        mixed = mixed.astype(BF16).astype(F32).reshape(frames, cols, chans)
        block_out[:, row] = (lat[:, row].astype(F32) + mixed).astype(BF16)
        for b in range(3):
            total = None
            for a in range(3):
                if 0 <= row - a + 1 < rows:
                    part = mm_t(pg[row - a + 1], ws[a, b])
                    total = part if total is None else total + part
            taps[b] = total

        @pl.loop(0, frames)
        def _(f):
            at = pl.ds(pl.multiple_of(f * cols, cols), cols)
            back = shift_left(taps[0, at]) + taps[1, at] + shift_right(taps[2, at])
            back_loc[row, at] = cot[f, row].astype(F32) + back


def last_kernel(above, below, back_loc, ws, latents_grad, taps):
    frames, rows, cols, chans = latents_grad.shape
    for row in range(rows):
        halos = []
        if row == 0:
            halos.append((2, above))
        if row == rows - 1:
            halos.append((0, below))
        for b in range(3):
            for n, (a, halo) in enumerate(halos):
                part = mm_t(halo[...], ws[a, b])
                taps[b] = part if n == 0 else taps[b] + part

        @pl.loop(0, frames)
        def _(f):
            at = pl.ds(pl.multiple_of(f * cols, cols), cols)
            back = back_loc[row, at]
            if halos:
                back += shift_left(taps[0, at]) + taps[1, at] + shift_right(taps[2, at])
            latents_grad[f, row] = back.astype(BF16)


def order_kernel(slots, code, sums, spatial, temporal, total):
    chans = spatial.shape[-1]
    size = total.shape[0] // slots
    for slot in range(slots):
        at = pl.multiple_of((slot ^ code[0]) * size, size)
        total[pl.ds(at, size)] = sums[slot * size : (slot + 1) * size].astype(F32)
    for a in range(3):
        for b in range(3):
            spatial[a, b] = total[a * chans : (a + 1) * chans, b * chans : (b + 1) * chans]
    for k in range(3):
        temporal[k] = total[3 * chans :, k * chans : (k + 1) * chans]


def partners(count):
    return [bit for bit in (1 << n for n in range(count.bit_length())) if bit < count]


def swap(x, axis, bit):
    return lax.ppermute(x, axis, [(i, i ^ bit) for i in range(lax.axis_size(axis))])


def plus(x, y):
    return (x.astype(F32) + y.astype(F32)).astype(BF16)


def stages(rows):
    steps = [("dp", bit) for bit in partners(lax.axis_size("dp"))]
    steps += [("tm", bit) for bit in partners(lax.axis_size("tm"))[1:]]
    steps += [("tm", 1)]
    halved = 0
    while halved < len(steps) and rows % (2 * TILE_ROWS << halved) == 0:
        halved += 1
    return steps, halved


def slot_code(steps, halved):
    code = 0
    for n, (axis, bit) in enumerate(steps[:halved]):
        mine = (lax.axis_index(axis) // bit) % 2
        code = code + mine * (1 << (halved - 1 - n))
    return code


def add_up(sums, steps, halved):
    for n, (axis, bit) in enumerate(steps):
        if n < halved:
            half = sums.shape[0] // 2
            sums = plus(sums[:half], swap(sums[half:], axis, bit))
        else:
            sums = plus(sums, swap(sums, axis, bit))
    for axis, bit in steps[:halved][::-1]:
        sums = jnp.concatenate([sums, swap(sums, axis, bit)], axis=0)
    return sums


def halo(first, last):
    ends = lax.axis_size("tm") - 1
    above = lax.ppermute(last, "tm", [(i, i + 1) for i in range(ends)])
    below = lax.ppermute(first, "tm", [(i + 1, i) for i in range(ends)])
    return above, below


def body(latents, cotangent, spatial_weight, temporal_weight):
    clips, frames, rows, cols, chans = latents.shape
    planes, shift = frames * clips, clips * cols
    cells = planes * cols
    lat = jnp.swapaxes(latents, 0, 1).reshape(planes, rows, cols, chans)
    cot = jnp.swapaxes(cotangent, 0, 1).reshape(planes, rows, cols, chans)
    scale = (clips * lax.axis_size("dp") * frames * rows * lax.axis_size("tm") * cols) ** (-0.5)
    steps, halved = stages(4 * chans)
    code = jnp.asarray(slot_code(steps, halved), jnp.int32).reshape(1)
    unit = 2 * cells * chans * chans

    above, below = halo(lat[:, 0].reshape(cells, chans), lat[:, rows - 1].reshape(cells, chans))
    wide = jax.ShapeDtypeStruct((rows, cells, chans), F32)
    narrow = jax.ShapeDtypeStruct((rows, cells, chans), BF16)
    taps = pltpu.VMEM((3, cells, chans), F32)
    padded = pltpu.VMEM((cells + 2 * shift, chans), BF16)
    pre_loc, act_grad = call(
        functools.partial(first_kernel, shift), [wide, narrow], [taps, padded], 56,
        (9 * rows - 6 + 3 * rows) * unit, lat, cot, spatial_weight, temporal_weight,
    )
    act, pg, sums = call(
        functools.partial(grads_kernel, shift, 1 << halved, scale),
        [narrow, narrow, jax.ShapeDtypeStruct((4 * chans, 3 * chans), BF16)],
        [
            taps,
            pltpu.VMEM((cells, 3 * chans), BF16),
            pltpu.VMEM((cells, 3 * chans), BF16),
            pltpu.VMEM((4 * chans, 3 * chans), F32),
        ],
        56, (6 + 12 * rows) * unit,
        code, lat, cot, above, below, pre_loc, act_grad, spatial_weight,
    )
    sums = add_up(sums, steps, halved)
    pg_above, pg_below = halo(pg[0], pg[rows - 1])
    image = jax.ShapeDtypeStruct(lat.shape, BF16)
    block_out, back_loc = call(
        functools.partial(out_kernel, shift), [image, wide], [taps, padded], 56,
        (9 * rows - 6 + 3 * rows) * unit, lat, cot, act, pg, spatial_weight, temporal_weight,
    )
    (latents_grad,) = call(
        last_kernel, [image], [taps], 56, 6 * unit, pg_above, pg_below, back_loc, spatial_weight
    )
    spatial_grad, temporal_grad = call(
        functools.partial(order_kernel, 1 << halved),
        [jax.ShapeDtypeStruct((3, 3, chans, chans), F32), jax.ShapeDtypeStruct((3, chans, chans), F32)],
        [pltpu.VMEM((4 * chans, 3 * chans), F32)], 40, 0, code, sums,
    )

    def back(x):
        return jnp.swapaxes(x.reshape(frames, clips, rows, cols, chans), 0, 1)

    return back(block_out), back(latents_grad), spatial_grad, temporal_grad


def solution(mesh):
    in_specs = (P("dp", None, "tm", None, None), P("dp", None, "tm", None, None), P(), P())
    out_specs = (P("dp", None, "tm", None, None), P("dp", None, "tm", None, None), P(), P())
    return jax.shard_map(body, mesh=mesh, in_specs=in_specs, out_specs=out_specs, check_vma=False)
```

```python
import functools
import itertools
import math

import jax
import jax.numpy as jnp
from jax import lax
from jax.experimental import pallas as pl
from jax.experimental.pallas import tpu as pltpu
from jax.sharding import PartitionSpec as P

BF16 = jnp.bfloat16
F32 = jnp.float32
TILE_ROWS = 16
LATENT_PARTS = (0.7,)
GRAD_PARTS = (0.4, 0.7)
VMEM = pl.BlockSpec(memory_space=pltpu.VMEM)
SMEM = pl.BlockSpec(memory_space=pltpu.SMEM)


def mm(a, b):
    return jnp.dot(a, b, preferred_element_type=F32)


def mm_t(a, b):
    return lax.dot_general(a, b, (((1,), (1,)), ((), ())), preferred_element_type=F32)


def outer(a, b):
    return lax.dot_general(a, b, (((0,), (0,)), ((), ())), preferred_element_type=F32)


def keep(x):
    return pltpu.with_memory_space_constraint(x, pltpu.VMEM)


def call(kernel, outs, scratch, vmem_mb, flops, args, aliases=None):
    size = sum(a.size * a.dtype.itemsize for a in args)
    size += sum(math.prod(o.shape) * jnp.dtype(o.dtype).itemsize for o in outs)
    return pl.pallas_call(
        kernel,
        out_shape=outs,
        in_specs=[SMEM if a.dtype == jnp.int32 else VMEM for a in args],
        out_specs=[VMEM] * len(outs),
        scratch_shapes=scratch,
        input_output_aliases=aliases or {},
        compiler_params=pltpu.CompilerParams(vmem_limit_bytes=vmem_mb << 20),
        cost_estimate=pl.CostEstimate(flops=flops, bytes_accessed=size, transcendentals=0),
    )(*args)


def shift_right(tile):
    w = lax.broadcasted_iota(jnp.int32, tile.shape, 0)
    return jnp.where(w == 0, 0.0, pltpu.roll(tile, 1, 0))


def shift_left(tile):
    w = lax.broadcasted_iota(jnp.int32, tile.shape, 0)
    last = tile.shape[0] - 1
    return jnp.where(w == last, 0.0, pltpu.roll(tile, last, 0))


def row_of(ref, row, first=0, last=None):
    planes, _, cols, chans = ref.shape
    last = planes if last is None else last
    return ref[first:last, row].reshape((last - first) * cols, chans)


def first_kernel(shift, lat, cot, ws, wt, pre_loc, act_grad, taps, cot_pad):
    planes, rows, cols, chans = lat.shape
    cells = planes * cols
    for row in range(rows):
        for b in range(3):
            total = None
            for a in range(3):
                if 0 <= row + a - 1 < rows:
                    part = mm(row_of(lat, row + a - 1), ws[a, b])
                    total = part if total is None else total + part
            taps[b] = total

        @pl.loop(0, planes)
        def _(f):
            at = pl.ds(pl.multiple_of(f * cols, cols), cols)
            pre_loc[row, at] = shift_right(taps[0, at]) + taps[1, at] + shift_left(taps[2, at])

        cot_pad[:cells] = row_of(cot, row)
        cot_pad[cells:] = jnp.zeros((2 * shift, chans), BF16)
        total = mm_t(cot_pad[:cells], wt[0])
        total += mm_t(cot_pad[pl.ds(shift, cells)], wt[1])
        total += mm_t(cot_pad[pl.ds(2 * shift, cells)], wt[2])
        act_grad[row] = total.astype(BF16)


def grads_kernel(part, rows, shift, ends, scale, *refs):
    first, last, final = part
    refs = list(refs)
    code = refs.pop(0) if final else None
    lat, cot, above, below, pre_loc, act_grad, ws = refs[:7]
    refs = refs[7:]
    before = refs.pop(0) if first else None
    acts, pgs, outs = refs[:rows], refs[rows : 2 * rows], refs[2 * rows : 2 * rows + (2 if final else 1)]
    taps, ext, spread, cots, total = refs[2 * rows + len(outs) :]
    planes, _, cols, chans = lat.shape
    cells, base = (last - first) * cols, first * cols
    ext[0] = above[...]
    ext[rows + 1] = below[...]
    for row in range(rows):
        ext[row + 1] = row_of(lat, row, first, last)
        halos = []
        if row == 0:
            halos.append((0, above))
        if row == rows - 1:
            halos.append((2, below))
        for b in range(3):
            for n, (a, halo) in enumerate(halos):
                out = mm(halo[...], ws[a, b])
                taps[b] = out if n == 0 else taps[b] + out

        @pl.loop(0, last - first)
        def _(f):
            at = pl.ds(pl.multiple_of(f * cols, cols), cols)
            whole = pl.ds(pl.multiple_of(base + f * cols, cols), cols)
            pre = pre_loc[row, whole]
            if halos:
                pre += shift_right(taps[0, at]) + taps[1, at] + shift_left(taps[2, at])
            sig = 1.0 / (1.0 + jnp.exp(-pre))
            act = pre * sig
            acts[row][at] = act.astype(BF16)
            grad = act_grad[row, whole].astype(F32) * sig * (1.0 + pre - act)
            grad16 = grad.astype(BF16)
            pgs[row][at] = grad16
            grad = grad16.astype(F32)
            spread[row, at, :chans] = shift_left(grad).astype(BF16)
            spread[row, at, chans : 2 * chans] = grad16
            spread[row, at, 2 * chans :] = shift_right(grad).astype(BF16)

        for k in range(3):
            skip = k * shift // cols
            there = min(last + skip, planes) - (first + skip)
            if there > 0:
                cots[row, : there * cols, k * chans : (k + 1) * chans] = row_of(cot, row, first + skip, first + skip + there)
            there = max(there, 0) * cols
            if there < cells:
                cots[row, there:, k * chans : (k + 1) * chans] = jnp.zeros((cells - there, chans), BF16)
    wide = rows * cells
    target = total if final else outs[0]
    for n in range(4):
        if n < 3:
            out = outer(ext[n : n + rows].reshape(wide, chans), spread[...].reshape(wide, 3 * chans))
        else:
            out = outer(jnp.concatenate([a[...] for a in acts], 0), cots[...].reshape(wide, 3 * chans))
        at = slice(n * chans, (n + 1) * chans)
        target[at] = out if before is None else before[at] + out
    if final:
        size = 2 * chans // ends
        for half in range(2):
            for slot in range(ends):
                at = (half ^ code[0]) * 2 * chans + (slot ^ code[1]) * size
                out = total[pl.ds(pl.multiple_of(at, size), size)] * scale
                outs[half][slot * size : (slot + 1) * size] = out.astype(BF16)


def out_kernel(shift, rows, parts, lat, *refs):
    acts, (wt, block_out, act_pad) = refs[:-3], refs[-3:]
    planes, rows, cols, chans = lat.shape
    cells = planes * cols
    for row in range(rows):
        act_pad[: 2 * shift] = jnp.zeros((2 * shift, chans), BF16)
        for n, (first, last) in enumerate(parts):
            act_pad[2 * shift + first * cols : 2 * shift + last * cols] = acts[n * rows + row][...]
        mixed = mm(act_pad[pl.ds(2 * shift, cells)], wt[0])
        mixed += mm(act_pad[pl.ds(shift, cells)], wt[1])
        mixed += mm(act_pad[:cells], wt[2])
        mixed = mixed.astype(BF16).astype(F32).reshape(planes, cols, chans)
        block_out[:, row] = (lat[:, row].astype(F32) + mixed).astype(BF16)


def back_kernel(rows, parts, cot, *refs):
    pgs, (ws, back_loc, taps) = refs[:-3], refs[-3:]
    _, _, cols, chans = cot.shape
    for row in range(rows):
        for n, (first, last) in enumerate(parts):
            at = slice(first * cols, last * cols)
            for b in range(3):
                total = None
                for a in range(3):
                    if 0 <= row - a + 1 < rows:
                        out = mm_t(pgs[n * rows + row - a + 1][...], ws[a, b])
                        total = out if total is None else total + out
                taps[b, at] = total

        @pl.loop(0, cot.shape[0])
        def _(f):
            at = pl.ds(pl.multiple_of(f * cols, cols), cols)
            back = shift_left(taps[0, at]) + taps[1, at] + shift_right(taps[2, at])
            back_loc[row, at] = cot[f, row].astype(F32) + back


def last_kernel(parts, back_loc, ws, *refs):
    aboves, belows = refs[: len(parts)], refs[len(parts) : 2 * len(parts)]
    latents_grad, taps = refs[2 * len(parts) :]
    planes, rows, cols, chans = latents_grad.shape
    for row in range(rows):
        halos = []
        if row == 0:
            halos.append((2, aboves))
        if row == rows - 1:
            halos.append((0, belows))
        for b in range(3):
            for n, (a, pieces) in enumerate(halos):
                for (first, last), piece in zip(parts, pieces):
                    at = slice(first * cols, last * cols)
                    out = mm_t(piece[...], ws[a, b])
                    taps[b, at] = out if n == 0 else taps[b, at] + out

        @pl.loop(0, planes)
        def _(f):
            at = pl.ds(pl.multiple_of(f * cols, cols), cols)
            back = back_loc[row, at]
            if halos:
                back += shift_left(taps[0, at]) + taps[1, at] + shift_right(taps[2, at])
            latents_grad[f, row] = back.astype(BF16)


def order_kernel(ends, code, mine, other, spatial, temporal, total):
    chans = spatial.shape[-1]
    size = 2 * chans // ends
    for half, sums in enumerate((mine, other)):
        for slot in range(ends):
            at = (half ^ code[0]) * 2 * chans + (slot ^ code[1]) * size
            total[pl.ds(pl.multiple_of(at, size), size)] = sums[slot * size : (slot + 1) * size].astype(F32)
    for a in range(3):
        for b in range(3):
            spatial[a, b] = total[a * chans : (a + 1) * chans, b * chans : (b + 1) * chans]
    for k in range(3):
        temporal[k] = total[3 * chans :, k * chans : (k + 1) * chans]


def bits_of(axis):
    count = lax.axis_size(axis)
    return [(axis, 1 << n) for n in range(count.bit_length()) if 1 << n < count]


def send(x, steps):
    wide, tall = lax.axis_size("dp"), lax.axis_size("tm")
    mask = sum(bit * tall if axis == "dp" else bit for axis, bit in steps)
    return lax.ppermute(x, ("dp", "tm"), [(i, i ^ mask) for i in range(wide * tall)])


def plus(x, *others):
    total = x.astype(F32)
    for other in others:
        total = total + other.astype(F32)
    return total.astype(BF16)


def groups_of(rows):
    wide, tall = bits_of("dp")[1:], bits_of("tm")
    order = [x for pair in zip(wide, tall[1:]) for x in pair]
    order += wide[len(tall) - 1 :] + tall[1 + len(wide) :] + tall[:1]
    groups, ends = [], 1
    while order:
        group, order = order[:2], order[2:]
        split = rows % (TILE_ROWS * ends << len(group)) == 0
        ends = ends << len(group) if split else ends
        groups.append((group, split))
    return groups, ends


def codes(groups):
    def bit_at(step):
        return (lax.axis_index(step[0]) // step[1]) % 2

    word = 0
    for group, split in groups:
        for step in group if split else ():
            word = 2 * word + bit_at(step)
    return jnp.stack([jnp.asarray(x, jnp.int32) for x in (bit_at(("dp", 1)), word)])


def subsets(group):
    return [[s for n, s in enumerate(group) if k >> (len(group) - 1 - n) & 1] for k in range(1, 1 << len(group))]


def add_up(mine, other, groups, beside, there, last):
    core = [("dp", 1)]
    mine = plus(mine, send(other, core))
    plan = [(group, split, True) for group, split in groups]
    plan += [(group, split, False) for group, split in reversed(groups) if split]
    for n, (group, split, down) in enumerate(plan):
        others = subsets(group)
        size = mine.shape[0] // (len(others) + 1) if split and down else 0
        got = [send(mine[(k + 1) * size : (k + 2) * size] if size else mine, steps) for k, steps in enumerate(others)]
        if n < len(plan) - 1:
            got, also = lax.optimization_barrier((got, beside[n]() if n < len(beside) else ()))
            there += [also] if also else []
        else:
            there += [run() for run in beside[n:]]
            got, end = lax.optimization_barrier((got, last()))
        mine = plus(mine[:size] if size else mine, *got) if down else jnp.concatenate([mine, *got], axis=0)
    return mine, send(mine, core), end


def halo(first, last):
    ends = lax.axis_size("tm") - 1
    above = lax.ppermute(last, "tm", [(i, i + 1) for i in range(ends)])
    below = lax.ppermute(first, "tm", [(i + 1, i) for i in range(ends)])
    return above, below


def body(latents, cotangent, spatial_weight, temporal_weight):
    clips, frames, rows, cols, chans = latents.shape
    planes, shift = frames * clips, clips * cols
    cells = planes * cols
    lat = jnp.swapaxes(latents, 0, 1).reshape(planes, rows, cols, chans)
    cot = jnp.swapaxes(cotangent, 0, 1).reshape(planes, rows, cols, chans)
    scale = (clips * lax.axis_size("dp") * frames * rows * lax.axis_size("tm") * cols) ** (-0.5)
    groups, ends = groups_of(2 * chans)
    code = codes(groups)
    unit = 2 * cells * chans * chans
    def cut(places):
        cuts = [0] + [round(planes * place) for place in places] + [planes]
        return list(zip(cuts[:-1], cuts[1:]))

    parts = cut(LATENT_PARTS)
    def ends_of(x, i, j):
        return x[i:j, 0].reshape(-1, chans), x[i:j, rows - 1].reshape(-1, chans)

    halos = [halo(*ends_of(lat, *parts[0]))]
    taps = pltpu.VMEM((3, cells, chans), F32)
    padded = pltpu.VMEM((cells + 2 * shift, chans), BF16)
    pre_loc, act_grad = call(
        functools.partial(first_kernel, shift),
        [pltpu.VMEM((rows, cells, chans), F32), pltpu.VMEM((rows, cells, chans), BF16)],
        [taps, padded], 28, (9 * rows - 6 + 3 * rows) * unit,
        [lat, cot, spatial_weight, temporal_weight],
    )
    rest, act_grad = lax.optimization_barrier((lat, act_grad))
    halos += [halo(*ends_of(rest, *part)) for part in parts[1:]]
    acts, pgs, total = [], [], None
    for n, (i, j) in enumerate(parts):
        final = n == len(parts) - 1
        size = (j - i) * cols
        narrow = jax.ShapeDtypeStruct((size, chans), BF16)
        if final:
            outs = [jax.ShapeDtypeStruct((2 * chans, 3 * chans), BF16)] * 2
        else:
            outs = [pltpu.VMEM((4 * chans, 3 * chans), F32)]
        args = [code] if final else []
        args += [keep(lat), keep(cot), keep(halos[n][0]), keep(halos[n][1]), keep(pre_loc), keep(act_grad)]
        args += [keep(spatial_weight)] + ([keep(total)] if n else [])
        done = call(
            functools.partial(grads_kernel, (i, j, final), rows, shift, ends, scale),
            [narrow] * (2 * rows) + outs,
            [
                pltpu.VMEM((3, size, chans), F32),
                pltpu.VMEM((rows + 2, size, chans), BF16),
                pltpu.VMEM((rows, size, 3 * chans), BF16),
                pltpu.VMEM((rows, size, 3 * chans), BF16),
                pltpu.VMEM((4 * chans, 3 * chans), F32),
            ],
            28, (6 + 12 * rows) * unit * (j - i) // planes, args,
        )
        acts += done[:rows]
        pgs += done[rows : 2 * rows]
        total = done[2 * rows]
    image = jax.ShapeDtypeStruct(lat.shape, BF16)
    grad_parts = cut(GRAD_PARTS)

    def grad_halo(i, j):
        def piece(row):
            found = [
                pgs[n * rows + row][(max(i, first) - first) * cols : (min(j, last) - first) * cols]
                for n, (first, last) in enumerate(parts)
                if max(i, first) < min(j, last)
            ]
            return found[0] if len(found) == 1 else jnp.concatenate(found, axis=0)

        return halo(piece(0), piece(rows - 1))

    def out():
        return call(
            functools.partial(out_kernel, shift, rows, parts), [image], [padded], 28, 3 * rows * unit,
            [lat, *acts, temporal_weight],
        )[0]

    def back():
        return call(
            functools.partial(back_kernel, rows, parts), [jax.ShapeDtypeStruct((rows, cells, chans), F32)], [taps], 28,
            (9 * rows - 6) * unit, [cot, *pgs, spatial_weight],
        )[0]

    works = [out, back]
    beside = [
        lambda part=part, work=work: (grad_halo(*part), work and work())
        for part, work in itertools.zip_longest(grad_parts, works)
    ]
    there = []

    def last():
        pg_halos = [pair for pair, _ in there]
        return call(
            functools.partial(last_kernel, grad_parts), [image], [taps], 28, 6 * unit,
            [there[1][1], spatial_weight, *(h[0] for h in pg_halos), *(h[1] for h in pg_halos)],
        )[0]

    mine, other, latents_grad = add_up(done[2 * rows], done[2 * rows + 1], groups, beside, there, last)
    block_out = there[0][1]
    spatial_grad, temporal_grad = call(
        functools.partial(order_kernel, ends),
        [jax.ShapeDtypeStruct((3, 3, chans, chans), F32), jax.ShapeDtypeStruct((3, chans, chans), F32)],
        [pltpu.VMEM((4 * chans, 3 * chans), F32)], 28, 0, [code, mine, other],
    )

    def home(x):
        return jnp.swapaxes(x.reshape(frames, clips, rows, cols, chans), 0, 1)

    return home(block_out), home(latents_grad), spatial_grad, temporal_grad


def solution(mesh):
    in_specs = (P("dp", None, "tm", None, None), P("dp", None, "tm", None, None), P(), P())
    out_specs = (P("dp", None, "tm", None, None), P("dp", None, "tm", None, None), P(), P())
    return jax.shard_map(body, mesh=mesh, in_specs=in_specs, out_specs=out_specs, check_vma=False)
```

```python
import functools
import itertools
import math

import jax
import jax.numpy as jnp
from jax import lax
from jax.experimental import pallas as pl
from jax.experimental.pallas import tpu as pltpu
from jax.sharding import PartitionSpec as P

BF16 = jnp.bfloat16
F32 = jnp.float32
TILE_ROWS = 16
PIECE_ROWS = 128
VMEM = pl.BlockSpec(memory_space=pltpu.VMEM)
SMEM = pl.BlockSpec(memory_space=pltpu.SMEM)
ANY = pl.BlockSpec(memory_space=pl.ANY)


def mm(a, b):
    return jnp.dot(a, b, preferred_element_type=F32)


def mm_t(a, b):
    return lax.dot_general(a, b, (((1,), (1,)), ((), ())), preferred_element_type=F32)


def outer(a, b):
    return lax.dot_general(a, b, (((0,), (0,)), ((), ())), preferred_element_type=F32)


def keep(x):
    return pltpu.with_memory_space_constraint(x, pltpu.VMEM)


def away(x):
    return pltpu.with_memory_space_constraint(x, pltpu.HBM)


def call(kernel, outs, scratch, vmem_mb, flops, args, far=(), out_far=False, aliases=None):
    size = sum(a.size * a.dtype.itemsize for a in args)
    size += sum(math.prod(o.shape) * jnp.dtype(o.dtype).itemsize for o in outs)
    args = [away(a) if n in far else a for n, a in enumerate(args)]
    specs = [SMEM if a.dtype == jnp.int32 else ANY if n in far else VMEM for n, a in enumerate(args)]
    return pl.pallas_call(
        kernel,
        out_shape=outs,
        in_specs=specs,
        out_specs=[ANY if out_far else VMEM] * len(outs),
        scratch_shapes=scratch,
        input_output_aliases=aliases or {},
        compiler_params=pltpu.CompilerParams(vmem_limit_bytes=vmem_mb << 20),
        cost_estimate=pl.CostEstimate(flops=flops, bytes_accessed=size, transcendentals=0),
    )(*args)


def start(src, dst, sem):
    copy = pltpu.make_async_copy(src, dst, sem)
    copy.start()
    return copy


def row_at(code, place, rows):
    return jnp.where(code[0] == 0, place, rows - 1 - place)


def tap_at(code, step):
    return jnp.where(code[0] == 0, 1 + step, 1 - step)


def shift_right(tile):
    w = lax.broadcasted_iota(jnp.int32, tile.shape, 0)
    return jnp.where(w == 0, 0.0, pltpu.roll(tile, 1, 0))


def shift_left(tile):
    w = lax.broadcasted_iota(jnp.int32, tile.shape, 0)
    last = tile.shape[0] - 1
    return jnp.where(w == last, 0.0, pltpu.roll(tile, last, 0))


def act_grad_kernel(shift, code, cot, wt, act_grad, cot_pad):
    planes, rows, cols, chans = cot.shape
    cells = planes * cols
    for place in range(rows):
        cot_pad[:cells] = cot[:, row_at(code, place, rows)].reshape(cells, chans)
        cot_pad[cells:] = jnp.zeros((2 * shift, chans), BF16)
        total = mm_t(cot_pad[:cells], wt[0])
        total += mm_t(cot_pad[pl.ds(shift, cells)], wt[1])
        total += mm_t(cot_pad[pl.ds(2 * shift, cells)], wt[2])
        act_grad[place] = total.astype(BF16)


def pre_kernel(code, lat, ws, pre_loc, taps):
    planes, rows, cols, chans = lat.shape
    cells = planes * cols
    for place in range(rows):
        for b in range(3):
            total = None
            for step in (-1, 0, 1):
                if 0 <= place + step < rows:
                    cells_in = lat[:, row_at(code, place + step, rows)].reshape(cells, chans)
                    part = mm(cells_in, ws[tap_at(code, step), b])
                    total = part if total is None else total + part
            taps[b] = total

        @pl.loop(0, planes)
        def _(f):
            at = pl.ds(pl.multiple_of(f * cols, cols), cols)
            pre_loc[place, at] = shift_right(taps[0, at]) + taps[1, at] + shift_left(taps[2, at])


def fetch(place, shift, code, lat, cot, pre_loc, act_grad, pres, grads, cots, sems):
    planes, rows, cols, chans = lat.shape
    row = row_at(code, place, rows)
    early = [start(pre_loc.at[place], pres, sems.at[0]), start(act_grad.at[place], grads, sems.at[1])]
    late = []
    for k in range(3):
        there, lanes = planes - k * shift // cols, slice(k * chans, (k + 1) * chans)
        src = cot.at[pl.ds(planes - there, there), row]
        late.append(start(src, cots.at[pl.ds(0, there), :, lanes], sems.at[2 + k]))
        if there < planes:
            cots[there:, :, lanes] = jnp.zeros((planes - there, cols, chans), BF16)
    return early, late


def point_grads(halo_taps, cols, taps, pres, grads, act_ref, pg_ref, spread):
    chans = pres.shape[-1]

    @pl.loop(0, pres.shape[0] // cols)
    def _(f):
        at = pl.ds(pl.multiple_of(f * cols, cols), cols)
        pre = pres[at]
        if halo_taps:
            pre += shift_right(taps[0, at]) + taps[1, at] + shift_left(taps[2, at])
        sig = 0.5 + 0.5 * jnp.tanh(0.5 * pre)
        act = pre * sig
        act_ref[at] = act.astype(BF16)
        grad = grads[at].astype(F32) * sig * (1.0 + pre - act)
        grad16 = grad.astype(BF16)
        pg_ref[at] = grad16
        spread[at, :chans] = shift_left(grad).astype(BF16)
        spread[at, chans : 2 * chans] = grad16
        spread[at, 2 * chans :] = shift_right(grad).astype(BF16)


def early_kernel(shift, code, lat, cot, halo, pre_loc, act_grad, ws, *refs):
    planes, rows, cols, chans = lat.shape
    cells, count = planes * cols, rows - 1
    acts, pgs, refs = refs[:count], refs[count : 2 * count], refs[2 * count :]
    sums, next_pres, next_grads, next_cots, next_ext, taps, ext, spread, cots, pres, grads, sems, next_sems = refs
    copies = []
    for n in range(count):
        copies.append(fetch(n, shift, code, lat, cot, pre_loc, act_grad, pres.at[n], grads.at[n], cots.at[n], sems.at[n]))
    rows_in = [start(lat.at[:, row_at(code, n, rows)], ext.at[n], sems.at[n, 5]) for n in range(rows)]
    ahead = sum(fetch(count, shift, code, lat, cot, pre_loc, act_grad, next_pres, next_grads, next_cots, next_sems), [])
    for n in range(2):
        ahead.append(start(lat.at[:, row_at(code, count - 1 + n, rows)], next_ext.at[n], next_sems.at[5 + n]))
    for b in range(3):
        taps[b] = mm(halo[...], ws[tap_at(code, -1), b])
    for n in range(count):
        for copy in copies[n][0]:
            copy.wait()
        point_grads(n == 0, cols, taps, pres.at[n], grads.at[n], acts[n], pgs[n], spread.at[n])
    for copy in rows_in + [copy for _, late in copies for copy in late]:
        copy.wait()
    for kind in range(4):
        out = None
        for n in range(count):
            if kind == 3:
                part = outer(acts[n][...], cots[n].reshape(cells, 3 * chans))
            elif kind + n == 0:
                part = outer(halo[...], spread[n])
            else:
                part = outer(ext[n + kind - 1].reshape(cells, chans), spread[n])
            out = part if out is None else out + part
        block = 3 if kind == 3 else tap_at(code, kind - 1)
        sums[pl.ds(pl.multiple_of(block * chans, chans), chans)] = out
    for copy in ahead:
        copy.wait()


def late_kernel(ends, scale, code, halo, ws, before, pres, grads, cots, ext, act, pg, sums, taps, spread):
    _, planes, cols, chans = ext.shape
    cells = planes * cols
    for b in range(3):
        taps[b] = mm(halo[...], ws[tap_at(code, 1), b])
    point_grads(True, cols, taps, pres, grads, act, pg, spread)
    size = 2 * chans // ends
    for kind in range(4):
        if kind == 3:
            out = outer(act[...], cots[...].reshape(cells, 3 * chans))
        elif kind == 2:
            out = outer(halo[...], spread[...])
        else:
            out = outer(ext[kind].reshape(cells, chans), spread[...])
        block = 3 if kind == 3 else tap_at(code, kind - 1)
        out = (before[pl.ds(pl.multiple_of(block * chans, chans), chans)] + out) * scale
        for n in range(chans // size):
            half, piece = lax.div(block, 2), lax.rem(block, 2) * (chans // size) + n
            here = pl.multiple_of((piece ^ code[2]) * size, size)
            sums[half ^ code[1], pl.ds(here, size)] = out[n * size : (n + 1) * size].astype(BF16)


def out_kernel(shift, code, lat, *refs):
    acts, (wt, block_out, act_pad) = refs[:-3], refs[-3:]
    planes, rows, cols, chans = lat.shape
    cells = planes * cols
    for place in range(rows):
        row = row_at(code, place, rows)
        act_pad[: 2 * shift] = jnp.zeros((2 * shift, chans), BF16)
        act_pad[2 * shift :] = acts[place][...]
        mixed = mm(act_pad[pl.ds(2 * shift, cells)], wt[0])
        mixed += mm(act_pad[pl.ds(shift, cells)], wt[1])
        mixed += mm(act_pad[:cells], wt[2])
        mixed = mixed.astype(BF16).astype(F32).reshape(planes, cols, chans)
        block_out[:, row] = (lat[:, row].astype(F32) + mixed).astype(BF16)


def back_kernel(code, cot, *refs):
    pgs, (ws, back_loc, taps) = refs[:-3], refs[-3:]
    planes, rows, cols, _ = cot.shape
    for place in range(rows):
        row = row_at(code, place, rows)
        for b in range(3):
            total = None
            for step in (-1, 0, 1):
                if 0 <= place - step < rows:
                    out = mm_t(pgs[place - step][...], ws[tap_at(code, step), b])
                    total = out if total is None else total + out
            taps[b] = total

        @pl.loop(0, planes)
        def _(f):
            at = pl.ds(pl.multiple_of(f * cols, cols), cols)
            back = shift_left(taps[0, at]) + taps[1, at] + shift_right(taps[2, at])
            back_loc[place, at] = cot[f, row].astype(F32) + back


def last_kernel(code, back_loc, ws, far, near, latents_grad, taps):
    planes, rows, cols, chans = latents_grad.shape
    for place in range(rows):
        row = row_at(code, place, rows)
        halos = [(1, far)] if place == 0 else []
        halos += [(-1, near)] if place == rows - 1 else []
        for n, (step, halo) in enumerate(halos):
            for b in range(3):
                out = mm_t(halo[...], ws[tap_at(code, step), b])
                taps[b] = out if n == 0 else taps[b] + out

        @pl.loop(0, planes)
        def _(f):
            at = pl.ds(pl.multiple_of(f * cols, cols), cols)
            back = back_loc[place, at]
            if halos:
                back += shift_left(taps[0, at]) + taps[1, at] + shift_right(taps[2, at])
            latents_grad[f, row] = back.astype(BF16)


def order_kernel(ends, own, code, sums, *refs):
    spatial, temporal, blocks, sems = refs[-4:]
    chans = spatial.shape[-1]
    size = 2 * chans // ends
    for slot in range(ends):
        piece = slot ^ code[2]
        block, at = lax.div(piece, chans // size), lax.rem(piece, chans // size) * size
        for b in range(3):
            found = sums[slot * size : (slot + 1) * size, b * chans : (b + 1) * chans]
            blocks[block, b, pl.ds(pl.multiple_of(at, size), size)] = found.astype(F32)
    half = code[1] if own else 1 - code[1]

    @pl.when(half == 0)
    def _():
        copies = [start(blocks.at[n], spatial.at[n], sems.at[n]) for n in range(2)]
        for copy in copies:
            copy.wait()

    @pl.when(half != 0)
    def _():
        copies = [start(blocks.at[0], spatial.at[2], sems.at[0]), start(blocks.at[1], temporal, sems.at[1])]
        for copy in copies:
            copy.wait()


def bits_of(axis):
    count = lax.axis_size(axis)
    return [(axis, 1 << n) for n in range(count.bit_length()) if 1 << n < count]


def send(x, steps):
    wide, tall = lax.axis_size("dp"), lax.axis_size("tm")
    mask = sum(bit * tall if axis == "dp" else bit for axis, bit in steps)
    return lax.ppermute(x, ("dp", "tm"), [(i, i ^ mask) for i in range(wide * tall)])


def send_pieces(x, steps):
    rows = x.shape[0]
    pieces = [send(x[n : min(n + PIECE_ROWS, rows)], steps) for n in range(0, rows, PIECE_ROWS)]
    return jnp.concatenate(pieces, axis=0) if len(pieces) > 1 else pieces[0]


def plus(x, *others):
    total = x.astype(F32)
    for other in others:
        total = total + other.astype(F32)
    return total.astype(BF16)


def groups_of(rows):
    wide, tall = bits_of("dp")[1:], bits_of("tm")
    groups, ends, split = [], 1, True
    for order, shared in ((wide, True), (tall[1:], True), (tall[:1], False)):
        while order:
            group, order = order[:2], order[2:]
            split = split and shared and rows % (TILE_ROWS * ends << len(group)) == 0
            ends = ends << len(group) if split else ends
            groups.append((group, split))
    return groups, ends


def codes(groups):
    def bit_at(step):
        return (lax.axis_index(step[0]) // step[1]) % 2

    word = 0
    for group, split in groups:
        for step in group if split else ():
            word = 2 * word + bit_at(step)
    return jnp.stack([jnp.asarray(x, jnp.int32) for x in (bit_at(("tm", 1)), bit_at(("dp", 1)), word)])


def subsets(group):
    return [[s for n, s in enumerate(group) if k >> (len(group) - 1 - n) & 1] for k in range(1, 1 << len(group))]


def add_up(mine, other, groups, beside, there):
    core = [("dp", 1)]
    mine = plus(mine, send_pieces(other, core))
    plan = [(group, split, True) for group, split in groups]
    shared = [step for group, split in groups if split for step in group]
    while shared:
        count = 2 - len(shared) % 2
        plan.append((shared[-count:], True, False))
        shared = shared[:-count]
    works = beside[: len(plan)]
    works[-1:] = [dict(itertools.chain.from_iterable(work.items() for work in beside[len(works) - 1 :]))]
    for n, (group, split, down) in enumerate(plan):
        others = subsets(group)
        size = mine.shape[0] // (len(others) + 1) if split and down else 0
        move = send_pieces if down else send
        got = [move(mine[(k + 1) * size : (k + 2) * size] if size else mine, steps) for k, steps in enumerate(others)]
        if n < len(works):
            got, also = lax.optimization_barrier((got, {name: run(mine) for name, run in works[n].items()}))
            there |= also
        mine = plus(mine[:size] if size else mine, *got) if down else jnp.concatenate([mine, *got], axis=0)
    return mine, send(mine, core)


def from_near(x):
    count = lax.axis_size("tm")
    return lax.ppermute(x, "tm", [(i, i ^ 1) for i in range(count) if i ^ 1 < count])


def from_far(x):
    count = lax.axis_size("tm")
    return lax.ppermute(x, "tm", [(i, j) for i in range(count) if 0 <= (j := ((i - 1) ^ 1) + 1) < count])


def after(x, *others):
    return lax.optimization_barrier((x, others))[0]


def body(latents, cotangent, spatial_weight, temporal_weight):
    clips, frames, rows, cols, chans = latents.shape
    planes, shift = frames * clips, clips * cols
    cells = planes * cols
    lat = jnp.swapaxes(latents, 0, 1).reshape(planes, rows, cols, chans)
    cot = jnp.swapaxes(cotangent, 0, 1).reshape(planes, rows, cols, chans)
    scale = (clips * lax.axis_size("dp") * frames * rows * lax.axis_size("tm") * cols) ** (-0.5)
    groups, ends = groups_of(2 * chans)
    code = codes(groups)
    unit = 2 * cells * chans * chans

    def lat_row(source, place):
        row = lax.axis_index("tm") % 2 * (rows - 1 - 2 * place) + place
        return lax.dynamic_index_in_dim(source, row, 1, keepdims=False).reshape(cells, chans)

    there = {}
    lat_far = from_far(lat_row(lat, 0))
    taps = pltpu.VMEM((3, cells, chans), F32)
    padded = pltpu.VMEM((cells + 2 * shift, chans), BF16)
    (act_grad,) = call(
        functools.partial(act_grad_kernel, shift), [pltpu.HBM((rows, cells, chans), BF16)], [padded], 10,
        3 * rows * unit, [code, cot, temporal_weight],
    )
    lat_near = from_near(lat_row(after(lat, act_grad), rows - 1))
    (pre_loc,) = call(
        pre_kernel, [pltpu.HBM((rows, cells, chans), F32)], [taps], 10, (9 * rows - 6) * unit,
        [code, after(lat, act_grad), spatial_weight],
    )
    narrow = jax.ShapeDtypeStruct((cells, chans), BF16)
    count = rows - 1
    early = call(
        functools.partial(early_kernel, shift),
        [narrow] * (2 * count)
        + [
            pltpu.VMEM((4 * chans, 3 * chans), F32),
            pltpu.VMEM((cells, chans), F32),
            pltpu.VMEM((cells, chans), BF16),
            pltpu.VMEM((planes, cols, 3 * chans), BF16),
            pltpu.VMEM((2, planes, cols, chans), BF16),
        ],
        [
            taps,
            pltpu.VMEM((rows, planes, cols, chans), BF16),
            pltpu.VMEM((count, cells, 3 * chans), BF16),
            pltpu.VMEM((count, planes, cols, 3 * chans), BF16),
            pltpu.VMEM((count, cells, chans), F32),
            pltpu.VMEM((count, cells, chans), BF16),
            pltpu.SemaphoreType.DMA((rows, 6)),
            pltpu.SemaphoreType.DMA((7,)),
        ],
        16, (3 + 12 * count) * unit, [code, lat, cot, keep(lat_far), pre_loc, act_grad, keep(spatial_weight)],
        far=(1, 2, 4, 5),
    )
    acts, pgs = list(early[:count]), list(early[count : 2 * count])
    there["far"] = from_far(after(pgs[0], lat_near))
    act, pg, sums = call(
        functools.partial(late_kernel, ends, scale),
        [narrow, narrow, jax.ShapeDtypeStruct((2, 2 * chans, 3 * chans), BF16)],
        [taps, pltpu.VMEM((cells, 3 * chans), BF16)], 12, 15 * unit,
        [code, *map(keep, (lat_near, spatial_weight, *early[2 * count :]))],
    )
    acts, pgs = acts + [act], pgs + [pg]
    image = jax.ShapeDtypeStruct(lat.shape, BF16)

    def out(_):
        return call(
            functools.partial(out_kernel, shift), [image], [padded], 12, 3 * rows * unit,
            [code, lat, *acts, temporal_weight],
        )[0]

    def back(_):
        return call(
            back_kernel, [jax.ShapeDtypeStruct((rows, cells, chans), F32)], [taps], 12,
            (9 * rows - 6) * unit, [code, cot, *pgs, spatial_weight],
        )[0]

    def last(_):
        return call(
            last_kernel, [image], [taps], 12, 6 * unit,
            [code, there["back"], keep(spatial_weight), keep(there["far"]), keep(there["near"])],
        )[0]

    def ordered(sums, *given):
        return call(
            functools.partial(order_kernel, ends, not given),
            [jax.ShapeDtypeStruct((3, 3, chans, chans), F32), jax.ShapeDtypeStruct((3, chans, chans), F32)],
            [pltpu.VMEM((2, 3, chans, chans), F32), pltpu.SemaphoreType.DMA((2,))],
            8, 0, [code, keep(sums), *given],
            far=(2, 3), out_far=True, aliases={2: 0, 3: 1} if given else None,
        )

    beside = [
        {"far": lambda _: there["far"], "out": out},
        {"near": lambda gate: from_near(after(pgs[-1], gate)), "back": back},
        {},
        {},
        {"last": last},
    ]
    mine, other = add_up(sums[0], sums[1], groups, beside, there)
    latents_grad, block_out = there["last"], there["out"]
    spatial_grad, temporal_grad = ordered(other, *ordered(mine))

    def home(x):
        return jnp.swapaxes(x.reshape(frames, clips, rows, cols, chans), 0, 1)

    return home(block_out), home(latents_grad), spatial_grad, temporal_grad


def solution(mesh):
    in_specs = (P("dp", None, "tm", None, None), P("dp", None, "tm", None, None), P(), P())
    out_specs = (P("dp", None, "tm", None, None), P("dp", None, "tm", None, None), P(), P())
    return jax.shard_map(body, mesh=mesh, in_specs=in_specs, out_specs=out_specs, check_vma=False)
```

```python
import functools
import math

import jax
import jax.numpy as jnp
from jax import lax
from jax.experimental import pallas as pl
from jax.experimental.pallas import tpu as pltpu
from jax.sharding import PartitionSpec as P

BF16 = jnp.bfloat16
F32 = jnp.float32
TILE_ROWS = 16
PIECE_ROWS = 128
VMEM = pl.BlockSpec(memory_space=pltpu.VMEM)
SMEM = pl.BlockSpec(memory_space=pltpu.SMEM)
ANY = pl.BlockSpec(memory_space=pl.ANY)


def mm(a, b):
    return jnp.dot(a, b, preferred_element_type=F32)


def mm_t(a, b):
    return lax.dot_general(a, b, (((1,), (1,)), ((), ())), preferred_element_type=F32)


def outer(a, b):
    return lax.dot_general(a, b, (((0,), (0,)), ((), ())), preferred_element_type=F32)


def keep(x):
    return pltpu.with_memory_space_constraint(x, pltpu.VMEM)


def away(x):
    return pltpu.with_memory_space_constraint(x, pltpu.HBM)


def call(kernel, outs, scratch, vmem_mb, flops, args, far=(), out_far=False, aliases=None):
    size = sum(a.size * a.dtype.itemsize for a in args)
    size += sum(math.prod(o.shape) * jnp.dtype(o.dtype).itemsize for o in outs)
    args = [away(a) if n in far else a for n, a in enumerate(args)]
    specs = [SMEM if a.dtype == jnp.int32 else ANY if n in far else VMEM for n, a in enumerate(args)]
    return pl.pallas_call(
        kernel,
        out_shape=outs,
        in_specs=specs,
        out_specs=[ANY if out_far else VMEM] * len(outs),
        scratch_shapes=scratch,
        input_output_aliases=aliases or {},
        compiler_params=pltpu.CompilerParams(vmem_limit_bytes=vmem_mb << 20),
        cost_estimate=pl.CostEstimate(flops=flops, bytes_accessed=size, transcendentals=0),
    )(*args)


def start(src, dst, sem):
    copy = pltpu.make_async_copy(src, dst, sem)
    copy.start()
    return copy


def row_at(code, place, rows):
    return jnp.where(code[0] == 0, place, rows - 1 - place)


def tap_at(code, step):
    return jnp.where(code[0] == 0, 1 + step, 1 - step)


def if_far(code, x):
    return x * code[3].astype(F32)


def shift_right(tile):
    w = lax.broadcasted_iota(jnp.int32, tile.shape, 0)
    return jnp.where(w == 0, 0.0, pltpu.roll(tile, 1, 0))


def shift_left(tile):
    w = lax.broadcasted_iota(jnp.int32, tile.shape, 0)
    last = tile.shape[0] - 1
    return jnp.where(w == last, 0.0, pltpu.roll(tile, last, 0))


def act_grad_kernel(shift, code, cot, wt, act_grad, cot_pad):
    planes, rows, cols, chans = cot.shape
    cells = planes * cols
    for place in range(rows):
        cot_pad[:cells] = cot[:, row_at(code, place, rows)].reshape(cells, chans)
        cot_pad[cells:] = jnp.zeros((2 * shift, chans), BF16)
        total = mm_t(cot_pad[:cells], wt[0])
        total += mm_t(cot_pad[pl.ds(shift, cells)], wt[1])
        total += mm_t(cot_pad[pl.ds(2 * shift, cells)], wt[2])
        act_grad[place] = total.astype(BF16)


def pre_kernel(code, lat, ws, pre_loc, taps):
    planes, rows, cols, chans = lat.shape
    cells = planes * cols
    for place in range(rows):
        for b in range(3):
            total = None
            for step in (-1, 0, 1):
                if 0 <= place + step < rows:
                    cells_in = lat[:, row_at(code, place + step, rows)].reshape(cells, chans)
                    part = mm(cells_in, ws[tap_at(code, step), b])
                    total = part if total is None else total + part
            taps[b] = total

        @pl.loop(0, planes)
        def _(f):
            at = pl.ds(pl.multiple_of(f * cols, cols), cols)
            pre_loc[place, at] = shift_right(taps[0, at]) + taps[1, at] + shift_left(taps[2, at])


def fetch(place, shift, code, lat, cot, pre_loc, act_grad, pres, grads, cots, sems):
    planes, rows, cols, chans = lat.shape
    row = row_at(code, place, rows)
    early = [start(pre_loc.at[place], pres, sems.at[0]), start(act_grad.at[place], grads, sems.at[1])]
    late = []
    for k in range(3):
        there, lanes = planes - k * shift // cols, slice(k * chans, (k + 1) * chans)
        src = cot.at[pl.ds(planes - there, there), row]
        late.append(start(src, cots.at[pl.ds(0, there), :, lanes], sems.at[2 + k]))
        if there < planes:
            cots[there:, :, lanes] = jnp.zeros((planes - there, cols, chans), BF16)
    return early, late


def point_grads(halo_taps, cols, taps, pres, grads, act_ref, pg_ref, spread):
    chans = pres.shape[-1]

    @pl.loop(0, pres.shape[0] // cols)
    def _(f):
        at = pl.ds(pl.multiple_of(f * cols, cols), cols)
        pre = pres[at]
        if halo_taps:
            pre += shift_right(taps[0, at]) + taps[1, at] + shift_left(taps[2, at])
        sig = 0.5 + 0.5 * jnp.tanh(0.5 * pre)
        act = pre * sig
        act_ref[at] = act.astype(BF16)
        grad = grads[at].astype(F32) * sig * (1.0 + pre - act)
        grad16 = grad.astype(BF16)
        pg_ref[at] = grad16
        spread[at, :chans] = shift_left(grad).astype(BF16)
        spread[at, chans : 2 * chans] = grad16
        spread[at, 2 * chans :] = shift_right(grad).astype(BF16)


def early_kernel(shift, code, lat, cot, halo, pre_loc, act_grad, ws, *refs):
    planes, rows, cols, chans = lat.shape
    cells, count = planes * cols, rows - 1
    acts, pgs, refs = refs[:count], refs[count : 2 * count], refs[2 * count :]
    sums, next_pres, next_grads, next_cots, next_ext, taps, ext, spread, cots, pres, grads, sems, next_sems = refs
    copies = []
    for n in range(count):
        copies.append(fetch(n, shift, code, lat, cot, pre_loc, act_grad, pres.at[n], grads.at[n], cots.at[n], sems.at[n]))
    rows_in = [start(lat.at[:, row_at(code, n, rows)], ext.at[n], sems.at[n, 5]) for n in range(rows)]
    ahead = sum(fetch(count, shift, code, lat, cot, pre_loc, act_grad, next_pres, next_grads, next_cots, next_sems), [])
    for n in range(2):
        ahead.append(start(lat.at[:, row_at(code, count - 1 + n, rows)], next_ext.at[n], next_sems.at[5 + n]))
    for b in range(3):
        taps[b] = if_far(code, mm(halo[...], ws[tap_at(code, -1), b]))
    for n in range(count):
        for copy in copies[n][0]:
            copy.wait()
        point_grads(n == 0, cols, taps, pres.at[n], grads.at[n], acts[n], pgs[n], spread.at[n])
    for copy in rows_in + [copy for _, late in copies for copy in late]:
        copy.wait()
    for kind in range(4):
        out = None
        for n in range(count):
            if kind == 3:
                part = outer(acts[n][...], cots[n].reshape(cells, 3 * chans))
            elif kind + n == 0:
                part = if_far(code, outer(halo[...], spread[n]))
            else:
                part = outer(ext[n + kind - 1].reshape(cells, chans), spread[n])
            out = part if out is None else out + part
        block = 3 if kind == 3 else tap_at(code, kind - 1)
        sums[pl.ds(pl.multiple_of(block * chans, chans), chans)] = out
    for copy in ahead:
        copy.wait()


def late_kernel(ends, scale, code, halo, ws, before, pres, grads, cots, ext, act, pg, sums, taps, spread):
    _, planes, cols, chans = ext.shape
    cells = planes * cols
    for b in range(3):
        taps[b] = mm(halo[...], ws[tap_at(code, 1), b])
    point_grads(True, cols, taps, pres, grads, act, pg, spread)
    size = 2 * chans // ends
    for kind in range(4):
        if kind == 3:
            out = outer(act[...], cots[...].reshape(cells, 3 * chans))
        elif kind == 2:
            out = outer(halo[...], spread[...])
        else:
            out = outer(ext[kind].reshape(cells, chans), spread[...])
        block = 3 if kind == 3 else tap_at(code, kind - 1)
        out = (before[pl.ds(pl.multiple_of(block * chans, chans), chans)] + out) * scale
        for n in range(chans // size):
            half, piece = lax.div(block, 2), lax.rem(block, 2) * (chans // size) + n
            here = pl.multiple_of((piece ^ code[2]) * size, size)
            sums[half ^ code[1], pl.ds(here, size)] = out[n * size : (n + 1) * size].astype(BF16)


def out_kernel(shift, code, lat, *refs):
    acts, (wt, block_out, act_pad) = refs[:-3], refs[-3:]
    planes, rows, cols, chans = lat.shape
    cells = planes * cols
    for place in range(rows):
        row = row_at(code, place, rows)
        act_pad[: 2 * shift] = jnp.zeros((2 * shift, chans), BF16)
        act_pad[2 * shift :] = acts[place][...]
        mixed = mm(act_pad[pl.ds(2 * shift, cells)], wt[0])
        mixed += mm(act_pad[pl.ds(shift, cells)], wt[1])
        mixed += mm(act_pad[:cells], wt[2])
        mixed = mixed.astype(BF16).astype(F32).reshape(planes, cols, chans)
        block_out[:, row] = (lat[:, row].astype(F32) + mixed).astype(BF16)


def back_kernel(code, cot, *refs):
    pgs, (ws, back_loc, taps) = refs[:-3], refs[-3:]
    planes, rows, cols, _ = cot.shape
    for place in range(rows):
        row = row_at(code, place, rows)
        for b in range(3):
            total = None
            for step in (-1, 0, 1):
                if 0 <= place - step < rows:
                    out = mm_t(pgs[place - step][...], ws[tap_at(code, step), b])
                    total = out if total is None else total + out
            taps[b] = total

        @pl.loop(0, planes)
        def _(f):
            at = pl.ds(pl.multiple_of(f * cols, cols), cols)
            back = shift_left(taps[0, at]) + taps[1, at] + shift_right(taps[2, at])
            back_loc[place, at] = cot[f, row].astype(F32) + back


def last_kernel(code, back_loc, ws, far, near, latents_grad, taps):
    planes, rows, cols, chans = latents_grad.shape
    for place in range(rows):
        row = row_at(code, place, rows)
        halos = [(1, far)] if place == 0 else []
        halos += [(-1, near)] if place == rows - 1 else []
        for n, (step, halo) in enumerate(halos):
            for b in range(3):
                out = mm_t(halo[...], ws[tap_at(code, step), b])
                out = if_far(code, out) if halo is far else out
                taps[b] = out if n == 0 else taps[b] + out

        @pl.loop(0, planes)
        def _(f):
            at = pl.ds(pl.multiple_of(f * cols, cols), cols)
            back = back_loc[place, at]
            if halos:
                back += shift_left(taps[0, at]) + taps[1, at] + shift_right(taps[2, at])
            latents_grad[f, row] = back.astype(BF16)


def order_kernel(ends, own, code, sums, *refs):
    spatial, temporal, blocks, sems = refs[-4:]
    chans = spatial.shape[-1]
    size = 2 * chans // ends
    for slot in range(ends):
        piece = slot ^ code[2]
        block, at = lax.div(piece, chans // size), lax.rem(piece, chans // size) * size
        for b in range(3):
            found = sums[slot * size : (slot + 1) * size, b * chans : (b + 1) * chans]
            blocks[block, b, pl.ds(pl.multiple_of(at, size), size)] = found.astype(F32)
    half = code[1] if own else 1 - code[1]

    @pl.when(half == 0)
    def _():
        copies = [start(blocks.at[n], spatial.at[n], sems.at[n]) for n in range(2)]
        for copy in copies:
            copy.wait()

    @pl.when(half != 0)
    def _():
        copies = [start(blocks.at[0], spatial.at[2], sems.at[0]), start(blocks.at[1], temporal, sems.at[1])]
        for copy in copies:
            copy.wait()


def bits_of(axis):
    count = lax.axis_size(axis)
    return [(axis, 1 << n) for n in range(count.bit_length()) if 1 << n < count]


def send(x, steps):
    wide, tall = lax.axis_size("dp"), lax.axis_size("tm")
    mask = sum(bit * tall if axis == "dp" else bit for axis, bit in steps)
    return lax.ppermute(x, ("dp", "tm"), [(i, i ^ mask) for i in range(wide * tall)])


def send_pieces(x, steps):
    rows = x.shape[0]
    pieces = [send(x[n : min(n + PIECE_ROWS, rows)], steps) for n in range(0, rows, PIECE_ROWS)]
    return jnp.concatenate(pieces, axis=0) if len(pieces) > 1 else pieces[0]


def plus(x, *others):
    total = x.astype(F32)
    for other in others:
        total = total + other.astype(F32)
    return total.astype(BF16)


def groups_of(rows):
    wide, tall = bits_of("dp")[1:], bits_of("tm")
    groups, ends, split = [], 1, True
    for order, shared in ((wide, True), (tall[1:], True), (tall[:1], False)):
        while order:
            group, order = order[:2], order[2:]
            split = split and shared and rows % (TILE_ROWS * ends << len(group)) == 0
            ends = ends << len(group) if split else ends
            groups.append((group, split))
    return groups, ends


def codes(groups):
    def bit_at(step):
        return (lax.axis_index(step[0]) // step[1]) % 2

    word = 0
    for group, split in groups:
        for step in group if split else ():
            word = 2 * word + bit_at(step)
    band = lax.axis_index("tm")
    has_far = jnp.where((band == 0) | (band == lax.axis_size("tm") - 1), 0, 1)
    return jnp.stack([jnp.asarray(x, jnp.int32) for x in (bit_at(("tm", 1)), bit_at(("dp", 1)), word, has_far)])


def subsets(group):
    return [[s for n, s in enumerate(group) if k >> (len(group) - 1 - n) & 1] for k in range(1, 1 << len(group))]


def add_up(mine, other, groups, beside, there):
    core = [("dp", 1)]
    mine = plus(mine, send_pieces(other, core))
    plan = [(group, split, True) for group, split in groups]
    shared = [step for group, split in groups if split for step in group]
    while shared:
        count = 2 - len(shared) % 2
        plan.append((shared[-count:], True, False))
        shared = shared[:-count]
    for n, (group, split, down) in enumerate(plan):
        others = subsets(group)
        size = mine.shape[0] // (len(others) + 1) if split and down else 0
        move = send_pieces if down else send
        got = [move(mine[(k + 1) * size : (k + 2) * size] if size else mine, steps) for k, steps in enumerate(others)]
        for run in beside[n : None if n == len(plan) - 1 else n + 1]:
            got, also = lax.optimization_barrier((got, run(mine)))
            there |= also
        mine = plus(mine[:size] if size else mine, *got) if down else jnp.concatenate([mine, *got], axis=0)
    return mine, send(mine, core)


def from_near(x):
    count = lax.axis_size("tm")
    return lax.ppermute(x, "tm", [(i, i ^ 1) for i in range(count) if i ^ 1 < count])


def from_far(x):
    wide, tall = lax.axis_size("dp"), lax.axis_size("tm")
    pairs = []
    for d in range(wide):
        for i in range(tall):
            j = ((i - 1) ^ 1) + 1
            pairs.append((d * tall + i, d * tall + j if 0 <= j < tall else (d ^ 1) * tall + i))
    return lax.ppermute(x, ("dp", "tm"), pairs)


def after(x, *others):
    return lax.optimization_barrier((x, others))[0]


def body(latents, cotangent, spatial_weight, temporal_weight):
    clips, frames, rows, cols, chans = latents.shape
    planes, shift = frames * clips, clips * cols
    cells = planes * cols
    lat = jnp.swapaxes(latents, 0, 1).reshape(planes, rows, cols, chans)
    cot = jnp.swapaxes(cotangent, 0, 1).reshape(planes, rows, cols, chans)
    scale = (clips * lax.axis_size("dp") * frames * rows * lax.axis_size("tm") * cols) ** (-0.5)
    groups, ends = groups_of(2 * chans)
    code = codes(groups)
    unit = 2 * cells * chans * chans

    def lat_row(source, place):
        row = lax.axis_index("tm") % 2 * (rows - 1 - 2 * place) + place
        return lax.dynamic_index_in_dim(source, row, 1, keepdims=False).reshape(cells, chans)

    there = {}
    lat_far = from_far(lat_row(lat, 0))
    taps = pltpu.VMEM((3, cells, chans), F32)
    padded = pltpu.VMEM((cells + 2 * shift, chans), BF16)
    (act_grad,) = call(
        functools.partial(act_grad_kernel, shift), [pltpu.HBM((rows, cells, chans), BF16)], [padded], 10,
        3 * rows * unit, [code, cot, temporal_weight],
    )
    lat_near = from_near(lat_row(after(lat, act_grad), rows - 1))
    (pre_loc,) = call(
        pre_kernel, [pltpu.HBM((rows, cells, chans), F32)], [taps], 10, (9 * rows - 6) * unit,
        [code, after(lat, act_grad), spatial_weight],
    )
    narrow = jax.ShapeDtypeStruct((cells, chans), BF16)
    count = rows - 1
    early = call(
        functools.partial(early_kernel, shift),
        [narrow] * (2 * count)
        + [
            pltpu.VMEM((4 * chans, 3 * chans), F32),
            pltpu.VMEM((cells, chans), F32),
            pltpu.VMEM((cells, chans), BF16),
            pltpu.VMEM((planes, cols, 3 * chans), BF16),
            pltpu.VMEM((2, planes, cols, chans), BF16),
        ],
        [
            taps,
            pltpu.VMEM((rows, planes, cols, chans), BF16),
            pltpu.VMEM((count, cells, 3 * chans), BF16),
            pltpu.VMEM((count, planes, cols, 3 * chans), BF16),
            pltpu.VMEM((count, cells, chans), F32),
            pltpu.VMEM((count, cells, chans), BF16),
            pltpu.SemaphoreType.DMA((rows, 6)),
            pltpu.SemaphoreType.DMA((7,)),
        ],
        16, (3 + 12 * count) * unit, [code, lat, cot, keep(lat_far), pre_loc, act_grad, keep(spatial_weight)],
        far=(1, 2, 4, 5),
    )
    acts, pgs = list(early[:count]), list(early[count : 2 * count])
    there["far"] = from_far(after(pgs[0], lat_near))
    act, pg, sums = call(
        functools.partial(late_kernel, ends, scale),
        [narrow, narrow, jax.ShapeDtypeStruct((2, 2 * chans, 3 * chans), BF16)],
        [taps, pltpu.VMEM((cells, 3 * chans), BF16)], 12, 15 * unit,
        [code, *map(keep, (lat_near, spatial_weight, *early[2 * count :]))],
    )
    acts, pgs = acts + [act], pgs + [pg]
    image = jax.ShapeDtypeStruct(lat.shape, BF16)

    def beside_first(gate):
        (block_out,) = call(
            functools.partial(out_kernel, shift), [image], [padded], 12, 3 * rows * unit,
            [code, lat, *acts, temporal_weight],
        )
        later.append(from_near(after(pgs[-1], gate)))
        return {"far": there["far"], "out": block_out}

    def beside_second(_):
        (back_loc,) = call(
            back_kernel, [jax.ShapeDtypeStruct((rows, cells, chans), F32)], [taps], 12,
            (9 * rows - 6) * unit, [code, cot, *pgs, spatial_weight],
        )
        return {"near": later[0], "back": back_loc}

    def beside_last(_):
        (latents_grad,) = call(
            last_kernel, [image], [taps], 12, 6 * unit,
            [code, there["back"], *map(keep, (spatial_weight, there["far"], there["near"]))],
        )
        return {"grad": latents_grad}

    def ordered(sums, *given):
        return call(
            functools.partial(order_kernel, ends, not given),
            [jax.ShapeDtypeStruct((3, 3, chans, chans), F32), jax.ShapeDtypeStruct((3, chans, chans), F32)],
            [pltpu.VMEM((2, 3, chans, chans), F32), pltpu.SemaphoreType.DMA((2,))],
            8, 0, [code, keep(sums), *given],
            far=(2, 3), out_far=True, aliases={2: 0, 3: 1} if given else None,
        )

    later = []
    beside = [beside_first, beside_second, lambda _: {}, lambda _: {}, beside_last]
    mine, other = add_up(sums[0], sums[1], groups, beside, there)
    block_out, latents_grad = there["out"], there["grad"]
    spatial_grad, temporal_grad = ordered(other, *ordered(mine))

    def home(x):
        return jnp.swapaxes(x.reshape(frames, clips, rows, cols, chans), 0, 1)

    return home(block_out), home(latents_grad), spatial_grad, temporal_grad


def solution(mesh):
    in_specs = (P("dp", None, "tm", None, None), P("dp", None, "tm", None, None), P(), P())
    out_specs = (P("dp", None, "tm", None, None), P("dp", None, "tm", None, None), P(), P())
    return jax.shard_map(body, mesh=mesh, in_specs=in_specs, out_specs=out_specs, check_vma=False)
```

```python
import functools
import math

import jax
import jax.numpy as jnp
from jax import lax
from jax.experimental import pallas as pl
from jax.experimental.pallas import tpu as pltpu
from jax.sharding import PartitionSpec as P

BF16 = jnp.bfloat16
F32 = jnp.float32
TILE_ROWS = 16
PIECE_ROWS = 512
VMEM = pl.BlockSpec(memory_space=pltpu.VMEM)
SMEM = pl.BlockSpec(memory_space=pltpu.SMEM)
ANY = pl.BlockSpec(memory_space=pl.ANY)


def mm(a, b):
    return jnp.dot(a, b, preferred_element_type=F32)


def mm_t(a, b):
    return lax.dot_general(a, b, (((1,), (1,)), ((), ())), preferred_element_type=F32)


def outer(a, b):
    return lax.dot_general(a, b, (((0,), (0,)), ((), ())), preferred_element_type=F32)


def keep(x):
    return pltpu.with_memory_space_constraint(x, pltpu.VMEM)


def away(x):
    return pltpu.with_memory_space_constraint(x, pltpu.HBM)


def call(kernel, outs, scratch, vmem_mb, flops, args, far=(), out_far=False, aliases=None):
    size = sum(a.size * a.dtype.itemsize for a in args)
    size += sum(math.prod(o.shape) * jnp.dtype(o.dtype).itemsize for o in outs)
    args = [away(a) if n in far else a for n, a in enumerate(args)]
    specs = [SMEM if a.dtype == jnp.int32 else ANY if n in far else VMEM for n, a in enumerate(args)]
    return pl.pallas_call(
        kernel,
        out_shape=outs,
        in_specs=specs,
        out_specs=[ANY if out_far else VMEM] * len(outs),
        scratch_shapes=scratch,
        input_output_aliases=aliases or {},
        compiler_params=pltpu.CompilerParams(vmem_limit_bytes=vmem_mb << 20),
        cost_estimate=pl.CostEstimate(flops=flops, bytes_accessed=size, transcendentals=0),
    )(*args)


def start(src, dst, sem):
    copy = pltpu.make_async_copy(src, dst, sem)
    copy.start()
    return copy


def row_at(code, place, rows):
    return jnp.where(code[0] == 0, place, rows - 1 - place)


def tap_at(code, step):
    return jnp.where(code[0] == 0, 1 + step, 1 - step)


def if_far(code, x):
    return x * code[3].astype(F32)


def shift_right(tile):
    w = lax.broadcasted_iota(jnp.int32, tile.shape, 0)
    return jnp.where(w == 0, 0.0, pltpu.roll(tile, 1, 0))


def shift_left(tile):
    w = lax.broadcasted_iota(jnp.int32, tile.shape, 0)
    last = tile.shape[0] - 1
    return jnp.where(w == last, 0.0, pltpu.roll(tile, last, 0))


def act_grad_kernel(shift, code, cot, wt, act_grad, cot_pad):
    planes, rows, cols, chans = cot.shape
    cells = planes * cols
    for place in range(rows):
        cot_pad[:cells] = cot[:, row_at(code, place, rows)].reshape(cells, chans)
        cot_pad[cells:] = jnp.zeros((2 * shift, chans), BF16)
        total = mm_t(cot_pad[:cells], wt[0])
        total += mm_t(cot_pad[pl.ds(shift, cells)], wt[1])
        total += mm_t(cot_pad[pl.ds(2 * shift, cells)], wt[2])
        act_grad[place] = total.astype(BF16)


def pre_kernel(code, lat, ws, pre_loc, taps):
    planes, rows, cols, chans = lat.shape
    cells = planes * cols
    for place in range(rows):
        for b in range(3):
            total = None
            for step in (-1, 0, 1):
                if 0 <= place + step < rows:
                    cells_in = lat[:, row_at(code, place + step, rows)].reshape(cells, chans)
                    part = mm(cells_in, ws[tap_at(code, step), b])
                    total = part if total is None else total + part
            taps[b] = total

        @pl.loop(0, planes)
        def _(f):
            at = pl.ds(pl.multiple_of(f * cols, cols), cols)
            pre_loc[place, at] = shift_right(taps[0, at]) + taps[1, at] + shift_left(taps[2, at])


def fetch(place, shift, code, lat, cot, pre_loc, act_grad, pres, grads, cots, sems):
    planes, rows, cols, chans = lat.shape
    row = row_at(code, place, rows)
    early = [start(pre_loc.at[place], pres, sems.at[0]), start(act_grad.at[place], grads, sems.at[1])]
    late = []
    for k in range(3):
        there, lanes = planes - k * shift // cols, slice(k * chans, (k + 1) * chans)
        src = cot.at[pl.ds(planes - there, there), row]
        late.append(start(src, cots.at[pl.ds(0, there), :, lanes], sems.at[2 + k]))
        if there < planes:
            cots[there:, :, lanes] = jnp.zeros((planes - there, cols, chans), BF16)
    return early, late


def point_grads(halo_taps, cols, taps, pres, grads, act_ref, pg_ref, spread):
    chans = pres.shape[-1]

    @pl.loop(0, pres.shape[0] // cols)
    def _(f):
        at = pl.ds(pl.multiple_of(f * cols, cols), cols)
        pre = pres[at]
        if halo_taps:
            pre += shift_right(taps[0, at]) + taps[1, at] + shift_left(taps[2, at])
        sig = 0.5 + 0.5 * jnp.tanh(0.5 * pre)
        act = pre * sig
        act_ref[at] = act.astype(BF16)
        grad = grads[at].astype(F32) * sig * (1.0 + pre - act)
        grad16 = grad.astype(BF16)
        pg_ref[at] = grad16
        spread[at, :chans] = shift_left(grad).astype(BF16)
        spread[at, chans : 2 * chans] = grad16
        spread[at, 2 * chans :] = shift_right(grad).astype(BF16)


def early_kernel(shift, code, lat, cot, halo, pre_loc, act_grad, ws, *refs):
    planes, rows, cols, chans = lat.shape
    cells, count = planes * cols, rows - 1
    acts, pgs, refs = refs[:count], refs[count : 2 * count], refs[2 * count :]
    sums, next_pres, next_grads, next_cots, next_ext, taps, ext, spread, cots, pres, grads, sems, next_sems = refs
    copies = []
    for n in range(count):
        copies.append(fetch(n, shift, code, lat, cot, pre_loc, act_grad, pres.at[n], grads.at[n], cots.at[n], sems.at[n]))
    rows_in = [start(lat.at[:, row_at(code, n, rows)], ext.at[n], sems.at[n, 5]) for n in range(rows)]
    ahead = sum(fetch(count, shift, code, lat, cot, pre_loc, act_grad, next_pres, next_grads, next_cots, next_sems), [])
    for n in range(2):
        ahead.append(start(lat.at[:, row_at(code, count - 1 + n, rows)], next_ext.at[n], next_sems.at[5 + n]))
    for b in range(3):
        taps[b] = if_far(code, mm(halo[...], ws[tap_at(code, -1), b]))
    for n in range(count):
        for copy in copies[n][0]:
            copy.wait()
        point_grads(n == 0, cols, taps, pres.at[n], grads.at[n], acts[n], pgs[n], spread.at[n])
    for copy in rows_in + [copy for _, late in copies for copy in late]:
        copy.wait()
    for kind in range(4):
        out = None
        for n in range(count):
            if kind == 3:
                part = outer(acts[n][...], cots[n].reshape(cells, 3 * chans))
            elif kind + n == 0:
                part = if_far(code, outer(halo[...], spread[n]))
            else:
                part = outer(ext[n + kind - 1].reshape(cells, chans), spread[n])
            out = part if out is None else out + part
        block = 3 if kind == 3 else tap_at(code, kind - 1)
        sums[pl.ds(pl.multiple_of(block * chans, chans), chans)] = out
    for copy in ahead:
        copy.wait()


def late_kernel(ends, scale, code, halo, ws, before, pres, grads, cots, ext, act, pg, spread, sums, taps):
    cols = ext.shape[2]
    for b in range(3):
        taps[b] = mm(halo[...], ws[tap_at(code, 1), b])
    point_grads(True, cols, taps, pres, grads, act, pg, spread)
    half_grads(ends, scale, 1 - code[1], code, halo, before, cots, ext, act, spread, sums)


def own_kernel(ends, scale, code, halo, before, cots, ext, act, spread, sums):
    half_grads(ends, scale, code[1], code, halo, before, cots, ext, act, spread, sums)


def half_grads(ends, scale, half, code, halo, before, cots, ext, act, spread, sums):
    _, planes, cols, chans = ext.shape
    cells = planes * cols
    size = 2 * chans // ends

    def put(block, a, b):
        at = block * chans
        out = (before[at : at + chans] + outer(a, b)) * scale
        for n in range(chans // size):
            here = pl.multiple_of(((block % 2 * (chans // size) + n) ^ code[2]) * size, size)
            sums[pl.ds(here, size)] = out[n * size : (n + 1) * size].astype(BF16)

    for odd in range(2):
        for side in range(2):

            @pl.when((code[0] == odd) & (half == side))
            def _():
                for block in (2 * side, 2 * side + 1):
                    if block == 3:
                        put(block, act[...], cots[...].reshape(cells, 3 * chans))
                        continue
                    kind = 2 - block if odd else block
                    put(block, halo[...] if kind == 2 else ext[kind].reshape(cells, chans), spread[...])


def out_kernel(shift, code, lat, *refs):
    acts, (wt, block_out, act_pad) = refs[:-3], refs[-3:]
    planes, rows, cols, chans = lat.shape
    cells = planes * cols
    for place in range(rows):
        row = row_at(code, place, rows)
        act_pad[: 2 * shift] = jnp.zeros((2 * shift, chans), BF16)
        act_pad[2 * shift :] = acts[place][...]
        mixed = mm(act_pad[pl.ds(2 * shift, cells)], wt[0])
        mixed += mm(act_pad[pl.ds(shift, cells)], wt[1])
        mixed += mm(act_pad[:cells], wt[2])
        mixed = mixed.astype(BF16).astype(F32).reshape(planes, cols, chans)
        block_out[:, row] = (lat[:, row].astype(F32) + mixed).astype(BF16)


def back_kernel(code, cot, *refs):
    pgs, (ws, back_loc, taps) = refs[:-3], refs[-3:]
    planes, rows, cols, _ = cot.shape
    for place in range(rows):
        row = row_at(code, place, rows)
        for b in range(3):
            total = None
            for step in (-1, 0, 1):
                if 0 <= place - step < rows:
                    out = mm_t(pgs[place - step][...], ws[tap_at(code, step), b])
                    total = out if total is None else total + out
            taps[b] = total

        @pl.loop(0, planes)
        def _(f):
            at = pl.ds(pl.multiple_of(f * cols, cols), cols)
            back = shift_left(taps[0, at]) + taps[1, at] + shift_right(taps[2, at])
            back_loc[place, at] = cot[f, row].astype(F32) + back


def last_kernel(code, back_loc, ws, far, near, latents_grad, taps):
    planes, rows, cols, chans = latents_grad.shape
    for place in range(rows):
        row = row_at(code, place, rows)
        halos = [(1, far)] if place == 0 else []
        halos += [(-1, near)] if place == rows - 1 else []
        for n, (step, halo) in enumerate(halos):
            for b in range(3):
                out = mm_t(halo[...], ws[tap_at(code, step), b])
                out = if_far(code, out) if halo is far else out
                taps[b] = out if n == 0 else taps[b] + out

        @pl.loop(0, planes)
        def _(f):
            at = pl.ds(pl.multiple_of(f * cols, cols), cols)
            back = back_loc[place, at]
            if halos:
                back += shift_left(taps[0, at]) + taps[1, at] + shift_right(taps[2, at])
            latents_grad[f, row] = back.astype(BF16)


def order_kernel(ends, own, code, sums, *refs):
    spatial, temporal, blocks, sems = refs[-4:]
    chans = spatial.shape[-1]
    size = 2 * chans // ends
    half = code[1] if own else 1 - code[1]
    first = pltpu.make_async_copy(blocks.at[0], spatial.at[2 * half], sems.at[0])
    second = pltpu.make_async_copy(blocks.at[1], spatial.at[1], sems.at[1])
    second_last = pltpu.make_async_copy(blocks.at[1], temporal, sems.at[1])
    for block in range(2):
        for n in range(chans // size):
            slot = (block * (chans // size) + n) ^ code[2]
            found = sums[pl.ds(pl.multiple_of(slot * size, size), size)].astype(F32)
            for b in range(3):
                blocks[block, b, n * size : (n + 1) * size] = found[:, b * chans : (b + 1) * chans]
        if block == 0:
            first.start()

    @pl.when(half == 0)
    def _():
        second.start()
        second.wait()

    @pl.when(half != 0)
    def _():
        second_last.start()
        second_last.wait()

    first.wait()


def bits_of(axis):
    count = lax.axis_size(axis)
    return [(axis, 1 << n) for n in range(count.bit_length()) if 1 << n < count]


def send(x, steps):
    wide, tall = lax.axis_size("dp"), lax.axis_size("tm")
    mask = sum(bit * tall if axis == "dp" else bit for axis, bit in steps)
    return lax.ppermute(x, ("dp", "tm"), [(i, i ^ mask) for i in range(wide * tall)])


def send_pieces(x, steps):
    rows = x.shape[0]
    pieces = [send(x[n : min(n + PIECE_ROWS, rows)], steps) for n in range(0, rows, PIECE_ROWS)]
    return jnp.concatenate(pieces, axis=0) if len(pieces) > 1 else pieces[0]


def plus(x, *others):
    total = x.astype(F32)
    for other in others:
        total = total + other.astype(F32)
    return total.astype(BF16)


def groups_of(rows):
    wide, tall = bits_of("dp")[1:], bits_of("tm")
    groups, ends, split = [], 1, True
    for order, shared in ((wide, True), (tall[1:], True), (tall[:1], False)):
        while order:
            group, order = order[:2], order[2:]
            split = split and shared and rows % (TILE_ROWS * ends << len(group)) == 0
            ends = ends << len(group) if split else ends
            groups.append((group, split))
    return groups, ends


def codes(groups):
    def bit_at(step):
        return (lax.axis_index(step[0]) // step[1]) % 2

    word = 0
    for group, split in groups:
        for step in group if split else ():
            word = 2 * word + bit_at(step)
    band = lax.axis_index("tm")
    has_far = jnp.where((band == 0) | (band == lax.axis_size("tm") - 1), 0, 1)
    return jnp.stack([jnp.asarray(x, jnp.int32) for x in (bit_at(("tm", 1)), bit_at(("dp", 1)), word, has_far)])


def subsets(group):
    return [[s for n, s in enumerate(group) if k >> (len(group) - 1 - n) & 1] for k in range(1, 1 << len(group))]


def add_up(mine, other, groups, beside, there):
    core = [("dp", 1)]
    mine = plus(mine, send_pieces(other, core))
    plan = [(group, split, True) for group, split in groups]
    shared = [step for group, split in groups if split for step in group]
    while shared:
        count = 2 - len(shared) % 2
        plan.append((shared[-count:], True, False))
        shared = shared[:-count]
    for n, (group, split, down) in enumerate(plan):
        others = subsets(group)
        size = mine.shape[0] // (len(others) + 1) if split and down else 0
        move = send_pieces if down else send
        got = [move(mine[(k + 1) * size : (k + 2) * size] if size else mine, steps) for k, steps in enumerate(others)]
        for run in beside[n : None if n == len(plan) - 1 else n + 1]:
            got, also = lax.optimization_barrier((got, run(mine)))
            there |= also
        mine = plus(mine[:size] if size else mine, *got) if down else jnp.concatenate([mine, *got], axis=0)
    return mine, send(mine, core)


def from_near(x):
    count = lax.axis_size("tm")
    return lax.ppermute(x, "tm", [(i, i ^ 1) for i in range(count) if i ^ 1 < count])


def from_far(x):
    wide, tall = lax.axis_size("dp"), lax.axis_size("tm")
    pairs = []
    for d in range(wide):
        for i in range(tall):
            j = ((i - 1) ^ 1) + 1
            pairs.append((d * tall + i, d * tall + j if 0 <= j < tall else (d ^ 1) * tall + i))
    return lax.ppermute(x, ("dp", "tm"), pairs)


def after(x, *others):
    return lax.optimization_barrier((x, others))[0]


def body(latents, cotangent, spatial_weight, temporal_weight):
    clips, frames, rows, cols, chans = latents.shape
    planes, shift = frames * clips, clips * cols
    cells = planes * cols
    lat = jnp.swapaxes(latents, 0, 1).reshape(planes, rows, cols, chans)
    cot = jnp.swapaxes(cotangent, 0, 1).reshape(planes, rows, cols, chans)
    scale = (clips * lax.axis_size("dp") * frames * rows * lax.axis_size("tm") * cols) ** (-0.5)
    groups, ends = groups_of(2 * chans)
    code = codes(groups)
    unit = 2 * cells * chans * chans

    def lat_row(source, place):
        row = lax.axis_index("tm") % 2 * (rows - 1 - 2 * place) + place
        return lax.dynamic_index_in_dim(source, row, 1, keepdims=False).reshape(cells, chans)

    there = {}
    lat_far = from_far(lat_row(lat, 0))
    taps = pltpu.VMEM((3, cells, chans), F32)
    padded = pltpu.VMEM((cells + 2 * shift, chans), BF16)
    (act_grad,) = call(
        functools.partial(act_grad_kernel, shift), [pltpu.HBM((rows, cells, chans), BF16)], [padded], 10,
        3 * rows * unit, [code, cot, temporal_weight],
    )
    lat_near = from_near(lat_row(after(lat, act_grad), rows - 1))
    (pre_loc,) = call(
        pre_kernel, [pltpu.HBM((rows, cells, chans), F32)], [taps], 10, (9 * rows - 6) * unit,
        [code, after(lat, act_grad), spatial_weight],
    )
    narrow = jax.ShapeDtypeStruct((cells, chans), BF16)
    count = rows - 1
    early = call(
        functools.partial(early_kernel, shift),
        [narrow] * (2 * count)
        + [
            pltpu.VMEM((4 * chans, 3 * chans), F32),
            pltpu.VMEM((cells, chans), F32),
            pltpu.VMEM((cells, chans), BF16),
            pltpu.VMEM((planes, cols, 3 * chans), BF16),
            pltpu.VMEM((2, planes, cols, chans), BF16),
        ],
        [
            taps,
            pltpu.VMEM((rows, planes, cols, chans), BF16),
            pltpu.VMEM((count, cells, 3 * chans), BF16),
            pltpu.VMEM((count, planes, cols, 3 * chans), BF16),
            pltpu.VMEM((count, cells, chans), F32),
            pltpu.VMEM((count, cells, chans), BF16),
            pltpu.SemaphoreType.DMA((rows, 6)),
            pltpu.SemaphoreType.DMA((7,)),
        ],
        16, (3 + 12 * count) * unit, [code, lat, cot, keep(lat_far), pre_loc, act_grad, keep(spatial_weight)],
        far=(1, 2, 4, 5),
    )
    acts, pgs = list(early[:count]), list(early[count : 2 * count])
    there["far"] = from_far(after(pgs[0], lat_near))
    half = pltpu.VMEM((2 * chans, 3 * chans), BF16)
    act, pg, spread, other = call(
        functools.partial(late_kernel, ends, scale),
        [narrow, narrow, pltpu.VMEM((cells, 3 * chans), BF16), half], [taps], 8, 9 * unit,
        [code, *map(keep, (lat_near, spatial_weight, *early[2 * count :]))],
    )
    (mine,) = call(
        functools.partial(own_kernel, ends, scale), [half], [], 8, 6 * unit,
        [code, *map(keep, (lat_near, early[2 * count], *early[2 * count + 3 :], act, spread))],
    )
    acts, pgs = acts + [act], pgs + [pg]
    image = jax.ShapeDtypeStruct(lat.shape, BF16)

    def beside_first(gate):
        (block_out,) = call(
            functools.partial(out_kernel, shift), [image], [padded], 12, 3 * rows * unit,
            [code, lat, *acts, temporal_weight],
        )
        later.append(from_near(after(pgs[-1], gate)))
        return {"far": there["far"], "out": block_out}

    def beside_second(_):
        (back_loc,) = call(
            back_kernel, [jax.ShapeDtypeStruct((rows, cells, chans), F32)], [taps], 12,
            (9 * rows - 6) * unit, [code, cot, *pgs, spatial_weight],
        )
        return {"near": later[0], "back": back_loc}

    def beside_last(_):
        (latents_grad,) = call(
            last_kernel, [image], [taps], 12, 6 * unit,
            [code, there["back"], *map(keep, (spatial_weight, there["far"], there["near"]))],
        )
        return {"grad": latents_grad}

    def ordered(sums, *given):
        return call(
            functools.partial(order_kernel, ends, not given),
            [jax.ShapeDtypeStruct((3, 3, chans, chans), F32), jax.ShapeDtypeStruct((3, chans, chans), F32)],
            [pltpu.VMEM((2, 3, chans, chans), F32), pltpu.SemaphoreType.DMA((2,))],
            8, 0, [code, keep(sums), *given],
            far=(2, 3), out_far=True, aliases={2: 0, 3: 1} if given else None,
        )

    later = []
    beside = [beside_first, beside_second, lambda _: {}, lambda _: {}, beside_last]
    mine, other = add_up(mine, other, groups, beside, there)
    block_out, latents_grad = there["out"], there["grad"]
    spatial_grad, temporal_grad = ordered(other, *ordered(mine))

    def home(x):
        return jnp.swapaxes(x.reshape(frames, clips, rows, cols, chans), 0, 1)

    return home(block_out), home(latents_grad), spatial_grad, temporal_grad


def solution(mesh):
    in_specs = (P("dp", None, "tm", None, None), P("dp", None, "tm", None, None), P(), P())
    out_specs = (P("dp", None, "tm", None, None), P("dp", None, "tm", None, None), P(), P())
    return jax.shard_map(body, mesh=mesh, in_specs=in_specs, out_specs=out_specs, check_vma=False)
```

```python
import functools
import math

import jax
import jax.numpy as jnp
from jax import lax
from jax.experimental import pallas as pl
from jax.experimental.pallas import tpu as pltpu
from jax.sharding import PartitionSpec as P

BF16 = jnp.bfloat16
F32 = jnp.float32
TILE_ROWS = 16
FAR_CUT, NEAR_CUT = 0.8, 0.7
PIECE_ROWS = 512
VMEM = pl.BlockSpec(memory_space=pltpu.VMEM)
SMEM = pl.BlockSpec(memory_space=pltpu.SMEM)
ANY = pl.BlockSpec(memory_space=pl.ANY)


def mm(a, b):
    return jnp.dot(a, b, preferred_element_type=F32)


def mm_t(a, b):
    return lax.dot_general(a, b, (((1,), (1,)), ((), ())), preferred_element_type=F32)


def outer(a, b):
    return lax.dot_general(a, b, (((0,), (0,)), ((), ())), preferred_element_type=F32)


def keep(x):
    return pltpu.with_memory_space_constraint(x, pltpu.VMEM)


def away(x):
    return pltpu.with_memory_space_constraint(x, pltpu.HBM)


def call(kernel, outs, scratch, vmem_mb, flops, args, far=(), out_far=False, aliases=None):
    size = sum(a.size * a.dtype.itemsize for a in args)
    size += sum(math.prod(o.shape) * jnp.dtype(o.dtype).itemsize for o in outs)
    args = [away(a) if n in far else a for n, a in enumerate(args)]
    specs = [SMEM if a.dtype == jnp.int32 else ANY if n in far else VMEM for n, a in enumerate(args)]
    return pl.pallas_call(
        kernel,
        out_shape=outs,
        in_specs=specs,
        out_specs=[ANY if out_far else VMEM] * len(outs),
        scratch_shapes=scratch,
        input_output_aliases=aliases or {},
        compiler_params=pltpu.CompilerParams(vmem_limit_bytes=vmem_mb << 20),
        cost_estimate=pl.CostEstimate(flops=flops, bytes_accessed=size, transcendentals=0),
    )(*args)


def start(src, dst, sem):
    copy = pltpu.make_async_copy(src, dst, sem)
    copy.start()
    return copy


def row_at(code, place, rows):
    return jnp.where(code[0] == 0, place, rows - 1 - place)


def tap_at(code, step):
    return jnp.where(code[0] == 0, 1 + step, 1 - step)


def if_far(code, x):
    return x * code[3].astype(F32)


def shift_right(tile):
    w = lax.broadcasted_iota(jnp.int32, tile.shape, 0)
    return jnp.where(w == 0, 0.0, pltpu.roll(tile, 1, 0))


def shift_left(tile):
    w = lax.broadcasted_iota(jnp.int32, tile.shape, 0)
    last = tile.shape[0] - 1
    return jnp.where(w == last, 0.0, pltpu.roll(tile, last, 0))


def act_grad_kernel(shift, code, cot, wt, act_grad, cot_pad):
    planes, rows, cols, chans = cot.shape
    cells = planes * cols
    for place in range(rows):
        cot_pad[:cells] = cot[:, row_at(code, place, rows)].reshape(cells, chans)
        cot_pad[cells:] = jnp.zeros((2 * shift, chans), BF16)
        total = mm_t(cot_pad[:cells], wt[0])
        total += mm_t(cot_pad[pl.ds(shift, cells)], wt[1])
        total += mm_t(cot_pad[pl.ds(2 * shift, cells)], wt[2])
        act_grad[place] = total.astype(BF16)


def pre_kernel(code, lat, ws, pre_loc, taps):
    planes, rows, cols, chans = lat.shape
    cells = planes * cols
    for place in range(rows):
        for b in range(3):
            total = None
            for step in (-1, 0, 1):
                if 0 <= place + step < rows:
                    cells_in = lat[:, row_at(code, place + step, rows)].reshape(cells, chans)
                    part = mm(cells_in, ws[tap_at(code, step), b])
                    total = part if total is None else total + part
            taps[b] = total

        @pl.loop(0, planes)
        def _(f):
            at = pl.ds(pl.multiple_of(f * cols, cols), cols)
            pre_loc[place, at] = shift_right(taps[0, at]) + taps[1, at] + shift_left(taps[2, at])


def fetch(place, shift, code, lat, cot, pre_loc, act_grad, pres, grads, cots, sems):
    planes, rows, cols, chans = lat.shape
    row = row_at(code, place, rows)
    early = [start(pre_loc.at[place], pres, sems.at[0]), start(act_grad.at[place], grads, sems.at[1])]
    late = []
    for k in range(3):
        there, lanes = planes - k * shift // cols, slice(k * chans, (k + 1) * chans)
        src = cot.at[pl.ds(planes - there, there), row]
        late.append(start(src, cots.at[pl.ds(0, there), :, lanes], sems.at[2 + k]))
        if there < planes:
            cots[there:, :, lanes] = jnp.zeros((planes - there, cols, chans), BF16)
    return early, late


def point_grads(halo_taps, cols, taps, pres, grads, act_ref, pg_ref, spread):
    chans = pres.shape[-1]

    @pl.loop(0, pres.shape[0] // cols)
    def _(f):
        at = pl.ds(pl.multiple_of(f * cols, cols), cols)
        pre = pres[at]
        if halo_taps:
            pre += shift_right(taps[0, at]) + taps[1, at] + shift_left(taps[2, at])
        sig = 0.5 + 0.5 * jnp.tanh(0.5 * pre)
        act = pre * sig
        act_ref[at] = act.astype(BF16)
        grad = grads[at].astype(F32) * sig * (1.0 + pre - act)
        grad16 = grad.astype(BF16)
        pg_ref[at] = grad16
        spread[at, :chans] = shift_left(grad).astype(BF16)
        spread[at, chans : 2 * chans] = grad16
        spread[at, 2 * chans :] = shift_right(grad).astype(BF16)


def early_kernel(shift, code, lat, cot, halo, pre_loc, act_grad, ws, *refs):
    planes, rows, cols, chans = lat.shape
    cells, count = planes * cols, rows - 1
    acts, pgs, refs = refs[:count], refs[count : 2 * count], refs[2 * count :]
    sums, next_pres, next_grads, next_cots, next_ext, taps, ext, spread, cots, pres, grads, sems, next_sems = refs
    copies = []
    for n in range(count):
        copies.append(fetch(n, shift, code, lat, cot, pre_loc, act_grad, pres.at[n], grads.at[n], cots.at[n], sems.at[n]))
    rows_in = [start(lat.at[:, row_at(code, n, rows)], ext.at[n], sems.at[n, 5]) for n in range(rows)]
    ahead = sum(fetch(count, shift, code, lat, cot, pre_loc, act_grad, next_pres, next_grads, next_cots, next_sems), [])
    for n in range(2):
        ahead.append(start(lat.at[:, row_at(code, count - 1 + n, rows)], next_ext.at[n], next_sems.at[5 + n]))
    for b in range(3):
        taps[b] = if_far(code, mm(halo[...], ws[tap_at(code, -1), b]))
    for n in range(count):
        for copy in copies[n][0]:
            copy.wait()
        point_grads(n == 0, cols, taps, pres.at[n], grads.at[n], acts[n], pgs[n], spread.at[n])
    for copy in rows_in + [copy for _, late in copies for copy in late]:
        copy.wait()
    for kind in range(4):
        out = None
        for n in range(count):
            if kind == 3:
                part = outer(acts[n][...], cots[n].reshape(cells, 3 * chans))
            elif kind + n == 0:
                part = if_far(code, outer(halo[...], spread[n]))
            else:
                part = outer(ext[n + kind - 1].reshape(cells, chans), spread[n])
            out = part if out is None else out + part
        block = 3 if kind == 3 else tap_at(code, kind - 1)
        sums[pl.ds(pl.multiple_of(block * chans, chans), chans)] = out
    for copy in ahead:
        copy.wait()


def late_kernel(ends, scale, code, halo, ws, before, pres, grads, cots, ext, act, pg, spread, sums, taps):
    cols = ext.shape[2]
    for b in range(3):
        taps[b] = mm(halo[...], ws[tap_at(code, 1), b])
    point_grads(True, cols, taps, pres, grads, act, pg, spread)
    half_grads(ends, scale, 1 - code[1], code, halo, before, cots, ext, act, spread, sums)


def own_kernel(ends, scale, code, halo, before, cots, ext, act, spread, sums):
    half_grads(ends, scale, code[1], code, halo, before, cots, ext, act, spread, sums)


def half_grads(ends, scale, half, code, halo, before, cots, ext, act, spread, sums):
    _, planes, cols, chans = ext.shape
    cells = planes * cols
    size = 2 * chans // ends

    def put(block, a, b):
        at = block * chans
        out = (before[at : at + chans] + outer(a, b)) * scale
        for n in range(chans // size):
            here = pl.multiple_of(((block % 2 * (chans // size) + n) ^ code[2]) * size, size)
            sums[pl.ds(here, size)] = out[n * size : (n + 1) * size].astype(BF16)

    for odd in range(2):
        for side in range(2):

            @pl.when((code[0] == odd) & (half == side))
            def _():
                for block in (2 * side, 2 * side + 1):
                    if block == 3:
                        put(block, act[...], cots[...].reshape(cells, 3 * chans))
                        continue
                    kind = 2 - block if odd else block
                    put(block, halo[...] if kind == 2 else ext[kind].reshape(cells, chans), spread[...])


def out_kernel(shift, code, lat, *refs):
    acts, (wt, block_out, act_pad) = refs[:-3], refs[-3:]
    planes, rows, cols, chans = lat.shape
    cells = planes * cols
    for place in range(rows):
        row = row_at(code, place, rows)
        act_pad[: 2 * shift] = jnp.zeros((2 * shift, chans), BF16)
        act_pad[2 * shift :] = acts[place][...]
        mixed = mm(act_pad[pl.ds(2 * shift, cells)], wt[0])
        mixed += mm(act_pad[pl.ds(shift, cells)], wt[1])
        mixed += mm(act_pad[:cells], wt[2])
        mixed = mixed.astype(BF16).astype(F32).reshape(planes, cols, chans)
        block_out[:, row] = (lat[:, row].astype(F32) + mixed).astype(BF16)


def back_kernel(code, cot, *refs):
    pgs, (ws, back_loc, taps) = refs[:-3], refs[-3:]
    planes, rows, cols, _ = cot.shape
    for place in range(rows):
        row = row_at(code, place, rows)
        for b in range(3):
            total = None
            for step in (-1, 0, 1):
                if 0 <= place - step < rows:
                    out = mm_t(pgs[place - step][...], ws[tap_at(code, step), b])
                    total = out if total is None else total + out
            taps[b] = total

        @pl.loop(0, planes)
        def _(f):
            at = pl.ds(pl.multiple_of(f * cols, cols), cols)
            back = shift_left(taps[0, at]) + taps[1, at] + shift_right(taps[2, at])
            back_loc[place, at] = cot[f, row].astype(F32) + back


def last_kernel(code, back_loc, ws, far_one, far_two, near_one, near_two, latents_grad, taps, both):
    planes, rows, cols, chans = latents_grad.shape
    far, near = both.at[0], both.at[1]
    for whole, one, two in ((far, far_one, far_two), (near, near_one, near_two)):
        cut = one.shape[0]
        whole[:cut] = one[...]
        whole[cut:] = two[...]
    for place in range(rows):
        row = row_at(code, place, rows)
        halos = [(1, far)] if place == 0 else []
        halos += [(-1, near)] if place == rows - 1 else []
        for n, (step, halo) in enumerate(halos):
            for b in range(3):
                out = mm_t(halo[...], ws[tap_at(code, step), b])
                out = if_far(code, out) if halo is far else out
                taps[b] = out if n == 0 else taps[b] + out

        @pl.loop(0, planes)
        def _(f):
            at = pl.ds(pl.multiple_of(f * cols, cols), cols)
            back = back_loc[place, at]
            if halos:
                back += shift_left(taps[0, at]) + taps[1, at] + shift_right(taps[2, at])
            latents_grad[f, row] = back.astype(BF16)


def order_kernel(ends, own, code, sums, *refs):
    spatial, temporal, blocks, sems = refs[-4:]
    chans = spatial.shape[-1]
    size = 2 * chans // ends
    half = code[1] if own else 1 - code[1]
    first = pltpu.make_async_copy(blocks.at[0], spatial.at[2 * half], sems.at[0])
    second = pltpu.make_async_copy(blocks.at[1], spatial.at[1], sems.at[1])
    second_last = pltpu.make_async_copy(blocks.at[1], temporal, sems.at[1])
    for block in range(2):
        for n in range(chans // size):
            slot = (block * (chans // size) + n) ^ code[2]
            found = sums[pl.ds(pl.multiple_of(slot * size, size), size)].astype(F32)
            for b in range(3):
                blocks[block, b, n * size : (n + 1) * size] = found[:, b * chans : (b + 1) * chans]
        if block == 0:
            first.start()

    @pl.when(half == 0)
    def _():
        second.start()
        second.wait()

    @pl.when(half != 0)
    def _():
        second_last.start()
        second_last.wait()

    first.wait()


def bits_of(axis):
    count = lax.axis_size(axis)
    return [(axis, 1 << n) for n in range(count.bit_length()) if 1 << n < count]


def send(x, steps):
    wide, tall = lax.axis_size("dp"), lax.axis_size("tm")
    mask = sum(bit * tall if axis == "dp" else bit for axis, bit in steps)
    return lax.ppermute(x, ("dp", "tm"), [(i, i ^ mask) for i in range(wide * tall)])


def send_pieces(x, steps):
    rows = x.shape[0]
    pieces = [send(x[n : min(n + PIECE_ROWS, rows)], steps) for n in range(0, rows, PIECE_ROWS)]
    return jnp.concatenate(pieces, axis=0) if len(pieces) > 1 else pieces[0]


def plus(x, *others):
    total = x.astype(F32)
    for other in others:
        total = total + other.astype(F32)
    return total.astype(BF16)


def groups_of(rows):
    wide, tall = bits_of("dp")[1:], bits_of("tm")
    groups, ends, split = [], 1, True
    for order, shared in ((wide, True), (tall[1:], True), (tall[:1], False)):
        while order:
            group, order = order[:2], order[2:]
            split = split and shared and rows % (TILE_ROWS * ends << len(group)) == 0
            ends = ends << len(group) if split else ends
            groups.append((group, split))
    return groups, ends


def codes(groups):
    def bit_at(step):
        return (lax.axis_index(step[0]) // step[1]) % 2

    word = 0
    for group, split in groups:
        for step in group if split else ():
            word = 2 * word + bit_at(step)
    band = lax.axis_index("tm")
    has_far = jnp.where((band == 0) | (band == lax.axis_size("tm") - 1), 0, 1)
    return jnp.stack([jnp.asarray(x, jnp.int32) for x in (bit_at(("tm", 1)), bit_at(("dp", 1)), word, has_far)])


def subsets(group):
    return [[s for n, s in enumerate(group) if k >> (len(group) - 1 - n) & 1] for k in range(1, 1 << len(group))]


def add_up(mine, other, groups, beside, there):
    core = [("dp", 1)]
    mine = plus(mine, send_pieces(other, core))
    plan = [(group, split, True) for group, split in groups]
    shared = [step for group, split in groups if split for step in group]
    while shared:
        count = 2 - len(shared) % 2
        plan.append((shared[-count:], True, False))
        shared = shared[:-count]
    for n, (group, split, down) in enumerate(plan):
        others = subsets(group)
        size = mine.shape[0] // (len(others) + 1) if split and down else 0
        move = send_pieces if down else send
        got = [move(mine[(k + 1) * size : (k + 2) * size] if size else mine, steps) for k, steps in enumerate(others)]
        for run in beside[n : None if n == len(plan) - 1 else n + 1]:
            got, also = lax.optimization_barrier((got, run(mine)))
            there |= also
        mine = plus(mine[:size] if size else mine, *got) if down else jnp.concatenate([mine, *got], axis=0)
    return mine, send(mine, core)


def from_near(x):
    count = lax.axis_size("tm")
    return lax.ppermute(x, "tm", [(i, i ^ 1) for i in range(count) if i ^ 1 < count])


def from_far(x):
    wide, tall = lax.axis_size("dp"), lax.axis_size("tm")
    pairs = []
    for d in range(wide):
        for i in range(tall):
            j = ((i - 1) ^ 1) + 1
            pairs.append((d * tall + i, d * tall + j if 0 <= j < tall else (d ^ 1) * tall + i))
    return lax.ppermute(x, ("dp", "tm"), pairs)


def after(x, *others):
    return lax.optimization_barrier((x, others))[0]


def body(latents, cotangent, spatial_weight, temporal_weight):
    clips, frames, rows, cols, chans = latents.shape
    planes, shift = frames * clips, clips * cols
    cells = planes * cols
    lat = jnp.swapaxes(latents, 0, 1).reshape(planes, rows, cols, chans)
    cot = jnp.swapaxes(cotangent, 0, 1).reshape(planes, rows, cols, chans)
    scale = (clips * lax.axis_size("dp") * frames * rows * lax.axis_size("tm") * cols) ** (-0.5)
    groups, ends = groups_of(2 * chans)
    code = codes(groups)
    unit = 2 * cells * chans * chans

    def lat_row(source, place):
        row = lax.axis_index("tm") % 2 * (rows - 1 - 2 * place) + place
        return lax.dynamic_index_in_dim(source, row, 1, keepdims=False).reshape(cells, chans)

    there = {}
    lat_far = from_far(lat_row(lat, 0))
    taps = pltpu.VMEM((3, cells, chans), F32)
    padded = pltpu.VMEM((cells + 2 * shift, chans), BF16)
    (act_grad,) = call(
        functools.partial(act_grad_kernel, shift), [pltpu.HBM((rows, cells, chans), BF16)], [padded], 10,
        3 * rows * unit, [code, cot, temporal_weight],
    )
    lat_near = from_near(lat_row(after(lat, act_grad), rows - 1))
    (pre_loc,) = call(
        pre_kernel, [pltpu.HBM((rows, cells, chans), F32)], [taps], 10, (9 * rows - 6) * unit,
        [code, after(lat, act_grad), spatial_weight],
    )
    narrow = jax.ShapeDtypeStruct((cells, chans), BF16)
    count = rows - 1
    early = call(
        functools.partial(early_kernel, shift),
        [narrow] * (2 * count)
        + [
            pltpu.VMEM((4 * chans, 3 * chans), F32),
            pltpu.VMEM((cells, chans), F32),
            pltpu.VMEM((cells, chans), BF16),
            pltpu.VMEM((planes, cols, 3 * chans), BF16),
            pltpu.VMEM((2, planes, cols, chans), BF16),
        ],
        [
            taps,
            pltpu.VMEM((rows, planes, cols, chans), BF16),
            pltpu.VMEM((count, cells, 3 * chans), BF16),
            pltpu.VMEM((count, planes, cols, 3 * chans), BF16),
            pltpu.VMEM((count, cells, chans), F32),
            pltpu.VMEM((count, cells, chans), BF16),
            pltpu.SemaphoreType.DMA((rows, 6)),
            pltpu.SemaphoreType.DMA((7,)),
        ],
        16, (3 + 12 * count) * unit, [code, lat, cot, keep(lat_far), pre_loc, act_grad, keep(spatial_weight)],
        far=(1, 2, 4, 5),
    )
    acts, pgs = list(early[:count]), list(early[count : 2 * count])
    cut, near_cut = (round(planes * part) * cols for part in (FAR_CUT, NEAR_CUT))
    there["far"] = from_far(after(pgs[0][:cut], lat_near))
    half = pltpu.VMEM((2 * chans, 3 * chans), BF16)
    act, pg, spread, other = call(
        functools.partial(late_kernel, ends, scale),
        [narrow, narrow, pltpu.VMEM((cells, 3 * chans), BF16), half], [taps], 8, 9 * unit,
        [code, *map(keep, (lat_near, spatial_weight, *early[2 * count :]))],
    )
    (mine,) = call(
        functools.partial(own_kernel, ends, scale), [half], [], 8, 6 * unit,
        [code, *map(keep, (lat_near, early[2 * count], *early[2 * count + 3 :], act, spread))],
    )
    acts, pgs = acts + [act], pgs + [pg]
    image = jax.ShapeDtypeStruct(lat.shape, BF16)

    def beside_first(gate):
        (block_out,) = call(
            functools.partial(out_kernel, shift), [image], [padded], 12, 3 * rows * unit,
            [code, lat, *acts, temporal_weight],
        )
        later.append(from_near(after(pgs[-1][:near_cut], gate)))
        later.append(from_far(after(pgs[0][cut:], gate)))
        return {"far": there["far"], "out": block_out}

    def beside_second(_):
        (back_loc,) = call(
            back_kernel, [jax.ShapeDtypeStruct((rows, cells, chans), F32)], [taps], 12,
            (9 * rows - 6) * unit, [code, cot, *pgs, spatial_weight],
        )
        return {"near": later[0], "back": back_loc, "rest": later[1]}

    def beside_fourth(gate):
        return {"last": from_near(after(pgs[-1][near_cut:], gate))}

    def beside_last(_):
        (latents_grad,) = call(
            last_kernel, [image], [taps, pltpu.VMEM((2, cells, chans), BF16)], 12, 6 * unit,
            [code, there["back"], keep(spatial_weight), *(keep(there[name]) for name in ("far", "rest", "near", "last"))],
        )
        return {"grad": latents_grad}

    def ordered(sums, *given):
        return call(
            functools.partial(order_kernel, ends, not given),
            [jax.ShapeDtypeStruct((3, 3, chans, chans), F32), jax.ShapeDtypeStruct((3, chans, chans), F32)],
            [pltpu.VMEM((2, 3, chans, chans), F32), pltpu.SemaphoreType.DMA((2,))],
            8, 0, [code, keep(sums), *given],
            far=(2, 3), out_far=True, aliases={2: 0, 3: 1} if given else None,
        )

    later = []
    beside = [beside_first, beside_second, lambda _: {}, beside_fourth, beside_last]
    mine, other = add_up(mine, other, groups, beside, there)
    block_out, latents_grad = there["out"], there["grad"]
    spatial_grad, temporal_grad = ordered(other, *ordered(mine))

    def home(x):
        return jnp.swapaxes(x.reshape(frames, clips, rows, cols, chans), 0, 1)

    return home(block_out), home(latents_grad), spatial_grad, temporal_grad


def solution(mesh):
    in_specs = (P("dp", None, "tm", None, None), P("dp", None, "tm", None, None), P(), P())
    out_specs = (P("dp", None, "tm", None, None), P("dp", None, "tm", None, None), P(), P())
    return jax.shard_map(body, mesh=mesh, in_specs=in_specs, out_specs=out_specs, check_vma=False)
```

```python
import functools
import math

import jax
import jax.numpy as jnp
from jax import lax
from jax.experimental import pallas as pl
from jax.experimental.pallas import tpu as pltpu
from jax.sharding import PartitionSpec as P

BF16 = jnp.bfloat16
F32 = jnp.float32
TILE_ROWS = 16
FAR_CUT, NEAR_CUT = 0.8, 0.7
PIECE_ROWS = 512
VMEM = pl.BlockSpec(memory_space=pltpu.VMEM)
SMEM = pl.BlockSpec(memory_space=pltpu.SMEM)
ANY = pl.BlockSpec(memory_space=pl.ANY)


def mm(a, b):
    return jnp.dot(a, b, preferred_element_type=F32)


def mm_t(a, b):
    return lax.dot_general(a, b, (((1,), (1,)), ((), ())), preferred_element_type=F32)


def outer(a, b):
    return lax.dot_general(a, b, (((0,), (0,)), ((), ())), preferred_element_type=F32)


def keep(x):
    return pltpu.with_memory_space_constraint(x, pltpu.VMEM)


def away(x):
    return pltpu.with_memory_space_constraint(x, pltpu.HBM)


def call(kernel, outs, scratch, vmem_mb, flops, args, far=(), out_far=False, aliases=None):
    size = sum(a.size * a.dtype.itemsize for a in args)
    size += sum(math.prod(o.shape) * jnp.dtype(o.dtype).itemsize for o in outs)
    args = [away(a) if n in far else a for n, a in enumerate(args)]
    specs = [SMEM if a.dtype == jnp.int32 else ANY if n in far else VMEM for n, a in enumerate(args)]
    return pl.pallas_call(
        kernel,
        out_shape=outs,
        in_specs=specs,
        out_specs=[ANY if out_far else VMEM] * len(outs),
        scratch_shapes=scratch,
        input_output_aliases=aliases or {},
        compiler_params=pltpu.CompilerParams(vmem_limit_bytes=vmem_mb << 20),
        cost_estimate=pl.CostEstimate(flops=flops, bytes_accessed=size, transcendentals=0),
    )(*args)


def start(src, dst, sem):
    copy = pltpu.make_async_copy(src, dst, sem)
    copy.start()
    return copy


def row_at(code, place, rows):
    return jnp.where(code[0] == 0, place, rows - 1 - place)


def tap_at(code, step):
    return jnp.where(code[0] == 0, 1 + step, 1 - step)


def if_far(code, x):
    return x * code[3].astype(F32)


def shift_right(tile):
    w = lax.broadcasted_iota(jnp.int32, tile.shape, 0)
    return jnp.where(w == 0, 0.0, pltpu.roll(tile, 1, 0))


def shift_left(tile):
    w = lax.broadcasted_iota(jnp.int32, tile.shape, 0)
    last = tile.shape[0] - 1
    return jnp.where(w == last, 0.0, pltpu.roll(tile, last, 0))


def act_grad_kernel(shift, code, cot, wt, act_grad, cot_pad):
    planes, rows, cols, chans = cot.shape
    cells = planes * cols
    for place in range(rows):
        cot_pad[:cells] = cot[:, row_at(code, place, rows)].reshape(cells, chans)
        cot_pad[cells:] = jnp.zeros((2 * shift, chans), BF16)
        total = mm_t(cot_pad[:cells], wt[0])
        total += mm_t(cot_pad[pl.ds(shift, cells)], wt[1])
        total += mm_t(cot_pad[pl.ds(2 * shift, cells)], wt[2])
        act_grad[place] = total.astype(BF16)


def pre_kernel(code, lat, ws, pre_loc, taps):
    planes, rows, cols, chans = lat.shape
    cells = planes * cols
    for place in range(rows):
        for b in range(3):
            total = None
            for step in (-1, 0, 1):
                if 0 <= place + step < rows:
                    cells_in = lat[:, row_at(code, place + step, rows)].reshape(cells, chans)
                    part = mm(cells_in, ws[tap_at(code, step), b])
                    total = part if total is None else total + part
            taps[b] = total

        @pl.loop(0, planes)
        def _(f):
            at = pl.ds(pl.multiple_of(f * cols, cols), cols)
            pre_loc[place, at] = shift_right(taps[0, at]) + taps[1, at] + shift_left(taps[2, at])


def fetch(place, shift, code, lat, cot, pre_loc, act_grad, pres, grads, cots, sems):
    planes, rows, cols, chans = lat.shape
    row = row_at(code, place, rows)
    early = [start(pre_loc.at[place], pres, sems.at[0]), start(act_grad.at[place], grads, sems.at[1])]
    late = []
    for k in range(3):
        there, lanes = planes - k * shift // cols, slice(k * chans, (k + 1) * chans)
        src = cot.at[pl.ds(planes - there, there), row]
        late.append(start(src, cots.at[pl.ds(0, there), :, lanes], sems.at[2 + k]))
        if there < planes:
            cots[there:, :, lanes] = jnp.zeros((planes - there, cols, chans), BF16)
    return early, late


def point_grads(halo_taps, cols, taps, pres, grads, act_ref, pg_ref, spread):
    chans = pres.shape[-1]

    @pl.loop(0, pres.shape[0] // cols, unroll=True)
    def _(f):
        at = pl.ds(pl.multiple_of(f * cols, cols), cols)
        pre = pres[at]
        if halo_taps:
            pre += shift_right(taps[0, at]) + taps[1, at] + shift_left(taps[2, at])
        sig = 0.5 + 0.5 * jnp.tanh(0.5 * pre)
        act = pre * sig
        act_ref[at] = act.astype(BF16)
        grad = grads[at].astype(F32) * sig * (1.0 + pre - act)
        grad16 = grad.astype(BF16)
        pg_ref[at] = grad16
        spread[at, :chans] = shift_left(grad).astype(BF16)
        spread[at, chans : 2 * chans] = grad16
        spread[at, 2 * chans :] = shift_right(grad).astype(BF16)


def early_kernel(shift, code, lat, cot, halo, pre_loc, act_grad, ws, *refs):
    planes, rows, cols, chans = lat.shape
    cells, count = planes * cols, rows - 1
    acts, pgs, refs = refs[:count], refs[count : 2 * count], refs[2 * count :]
    sums, next_pres, next_grads, next_cots, next_ext, taps, ext, spread, cots, pres, grads, sems, next_sems = refs
    copies = []
    for n in range(count):
        copies.append(fetch(n, shift, code, lat, cot, pre_loc, act_grad, pres.at[n], grads.at[n], cots.at[n], sems.at[n]))
    rows_in = [start(lat.at[:, row_at(code, n, rows)], ext.at[n], sems.at[n, 5]) for n in range(rows)]
    ahead = sum(fetch(count, shift, code, lat, cot, pre_loc, act_grad, next_pres, next_grads, next_cots, next_sems), [])
    for n in range(2):
        ahead.append(start(lat.at[:, row_at(code, count - 1 + n, rows)], next_ext.at[n], next_sems.at[5 + n]))
    for b in range(3):
        taps[b] = if_far(code, mm(halo[...], ws[tap_at(code, -1), b]))
    for n in range(count):
        for copy in copies[n][0]:
            copy.wait()
        point_grads(n == 0, cols, taps, pres.at[n], grads.at[n], acts[n], pgs[n], spread.at[n])
    for copy in rows_in + [copy for _, late in copies for copy in late]:
        copy.wait()
    for kind in range(4):
        out = None
        for n in range(count):
            if kind == 3:
                part = outer(acts[n][...], cots[n].reshape(cells, 3 * chans))
            elif kind + n == 0:
                part = if_far(code, outer(halo[...], spread[n]))
            else:
                part = outer(ext[n + kind - 1].reshape(cells, chans), spread[n])
            out = part if out is None else out + part
        block = 3 if kind == 3 else tap_at(code, kind - 1)
        sums[pl.ds(pl.multiple_of(block * chans, chans), chans)] = out
    for copy in ahead:
        copy.wait()


def late_kernel(ends, scale, code, halo, ws, before, pres, grads, cots, ext, act, pg, spread, sums, taps):
    cols = ext.shape[2]
    for b in range(3):
        taps[b] = mm(halo[...], ws[tap_at(code, 1), b])
    point_grads(True, cols, taps, pres, grads, act, pg, spread)
    half_grads(ends, scale, 1 - code[1], code, halo, before, cots, ext, act, spread, sums)


def own_kernel(ends, scale, code, halo, before, cots, ext, act, spread, sums):
    half_grads(ends, scale, code[1], code, halo, before, cots, ext, act, spread, sums)


def half_grads(ends, scale, half, code, halo, before, cots, ext, act, spread, sums):
    _, planes, cols, chans = ext.shape
    cells = planes * cols
    size = 2 * chans // ends

    def put(block, a, b):
        at = block * chans
        out = (before[at : at + chans] + outer(a, b)) * scale
        for n in range(chans // size):
            here = pl.multiple_of(((block % 2 * (chans // size) + n) ^ code[2]) * size, size)
            sums[pl.ds(here, size)] = out[n * size : (n + 1) * size].astype(BF16)

    for odd in range(2):
        for side in range(2):

            @pl.when((code[0] == odd) & (half == side))
            def _():
                for block in (2 * side, 2 * side + 1):
                    if block == 3:
                        put(block, act[...], cots[...].reshape(cells, 3 * chans))
                        continue
                    kind = 2 - block if odd else block
                    put(block, halo[...] if kind == 2 else ext[kind].reshape(cells, chans), spread[...])


def out_kernel(shift, code, lat, *refs):
    acts, (wt, block_out, act_pad) = refs[:-3], refs[-3:]
    planes, rows, cols, chans = lat.shape
    cells = planes * cols
    for place in range(rows):
        row = row_at(code, place, rows)
        act_pad[: 2 * shift] = jnp.zeros((2 * shift, chans), BF16)
        act_pad[2 * shift :] = acts[place][...]
        mixed = mm(act_pad[pl.ds(2 * shift, cells)], wt[0])
        mixed += mm(act_pad[pl.ds(shift, cells)], wt[1])
        mixed += mm(act_pad[:cells], wt[2])
        mixed = mixed.astype(BF16).astype(F32).reshape(planes, cols, chans)
        block_out[:, row] = (lat[:, row].astype(F32) + mixed).astype(BF16)


def back_kernel(code, cot, *refs):
    pgs, (ws, back_loc, taps) = refs[:-3], refs[-3:]
    planes, rows, cols, _ = cot.shape
    for place in range(rows):
        row = row_at(code, place, rows)
        for b in range(3):
            total = None
            for step in (-1, 0, 1):
                if 0 <= place - step < rows:
                    out = mm_t(pgs[place - step][...], ws[tap_at(code, step), b])
                    total = out if total is None else total + out
            taps[b] = total

        @pl.loop(0, planes)
        def _(f):
            at = pl.ds(pl.multiple_of(f * cols, cols), cols)
            back = shift_left(taps[0, at]) + taps[1, at] + shift_right(taps[2, at])
            back_loc[place, at] = cot[f, row].astype(F32) + back


def last_kernel(code, back_loc, ws, far_one, far_two, near_one, near_two, latents_grad, taps, both):
    planes, rows, cols, chans = latents_grad.shape
    far, near = both.at[0], both.at[1]
    for whole, one, two in ((far, far_one, far_two), (near, near_one, near_two)):
        cut = one.shape[0]
        whole[:cut] = one[...]
        whole[cut:] = two[...]
    for place in range(rows):
        row = row_at(code, place, rows)
        halos = [(1, far)] if place == 0 else []
        halos += [(-1, near)] if place == rows - 1 else []
        for n, (step, halo) in enumerate(halos):
            for b in range(3):
                out = mm_t(halo[...], ws[tap_at(code, step), b])
                out = if_far(code, out) if halo is far else out
                taps[b] = out if n == 0 else taps[b] + out

        @pl.loop(0, planes)
        def _(f):
            at = pl.ds(pl.multiple_of(f * cols, cols), cols)
            back = back_loc[place, at]
            if halos:
                back += shift_left(taps[0, at]) + taps[1, at] + shift_right(taps[2, at])
            latents_grad[f, row] = back.astype(BF16)


def order_kernel(ends, own, code, sums, *refs):
    spatial, temporal, blocks, sems = refs[-4:]
    chans = spatial.shape[-1]
    size = 2 * chans // ends
    half = code[1] if own else 1 - code[1]
    first = pltpu.make_async_copy(blocks.at[0], spatial.at[2 * half], sems.at[0])
    second = pltpu.make_async_copy(blocks.at[1], spatial.at[1], sems.at[1])
    second_last = pltpu.make_async_copy(blocks.at[1], temporal, sems.at[1])
    for block in range(2):
        for n in range(chans // size):
            slot = (block * (chans // size) + n) ^ code[2]
            found = sums[pl.ds(pl.multiple_of(slot * size, size), size)].astype(F32)
            for b in range(3):
                blocks[block, b, n * size : (n + 1) * size] = found[:, b * chans : (b + 1) * chans]
        if block == 0:
            first.start()

    @pl.when(half == 0)
    def _():
        second.start()
        second.wait()

    @pl.when(half != 0)
    def _():
        second_last.start()
        second_last.wait()

    first.wait()


def bits_of(axis):
    count = lax.axis_size(axis)
    return [(axis, 1 << n) for n in range(count.bit_length()) if 1 << n < count]


def send(x, steps):
    wide, tall = lax.axis_size("dp"), lax.axis_size("tm")
    mask = sum(bit * tall if axis == "dp" else bit for axis, bit in steps)
    return lax.ppermute(x, ("dp", "tm"), [(i, i ^ mask) for i in range(wide * tall)])


def send_pieces(x, steps):
    rows = x.shape[0]
    pieces = [send(x[n : min(n + PIECE_ROWS, rows)], steps) for n in range(0, rows, PIECE_ROWS)]
    return jnp.concatenate(pieces, axis=0) if len(pieces) > 1 else pieces[0]


def plus(x, *others):
    total = x.astype(F32)
    for other in others:
        total = total + other.astype(F32)
    return total.astype(BF16)


def groups_of(rows):
    wide, tall = bits_of("dp")[1:], bits_of("tm")
    groups, ends, split = [], 1, True
    for order, shared in ((wide, True), (tall[1:], True), (tall[:1], False)):
        while order:
            group, order = order[:2], order[2:]
            split = split and shared and rows % (TILE_ROWS * ends << len(group)) == 0
            ends = ends << len(group) if split else ends
            groups.append((group, split))
    return groups, ends


def codes(groups):
    def bit_at(step):
        return (lax.axis_index(step[0]) // step[1]) % 2

    word = 0
    for group, split in groups:
        for step in group if split else ():
            word = 2 * word + bit_at(step)
    band = lax.axis_index("tm")
    has_far = jnp.where((band == 0) | (band == lax.axis_size("tm") - 1), 0, 1)
    return jnp.stack([jnp.asarray(x, jnp.int32) for x in (bit_at(("tm", 1)), bit_at(("dp", 1)), word, has_far)])


def subsets(group):
    return [[s for n, s in enumerate(group) if k >> (len(group) - 1 - n) & 1] for k in range(1, 1 << len(group))]


def add_up(mine, other, groups, beside, there):
    core = [("dp", 1)]
    mine = plus(mine, send_pieces(other, core))
    plan = [(group, split, True) for group, split in groups]
    shared = [step for group, split in groups if split for step in group]
    while shared:
        count = 2 - len(shared) % 2
        plan.append((shared[-count:], True, False))
        shared = shared[:-count]
    for n, (group, split, down) in enumerate(plan):
        others = subsets(group)
        size = mine.shape[0] // (len(others) + 1) if split and down else 0
        move = send_pieces if down else send
        got = [move(mine[(k + 1) * size : (k + 2) * size] if size else mine, steps) for k, steps in enumerate(others)]
        for run in beside[n : None if n == len(plan) - 1 else n + 1]:
            got, also = lax.optimization_barrier((got, run(mine)))
            there |= also
        mine = plus(mine[:size] if size else mine, *got) if down else jnp.concatenate([mine, *got], axis=0)
    return mine, send(mine, core)


def from_near(x):
    count = lax.axis_size("tm")
    return lax.ppermute(x, "tm", [(i, i ^ 1) for i in range(count) if i ^ 1 < count])


def from_far(x):
    wide, tall = lax.axis_size("dp"), lax.axis_size("tm")
    pairs = []
    for d in range(wide):
        for i in range(tall):
            j = ((i - 1) ^ 1) + 1
            pairs.append((d * tall + i, d * tall + j if 0 <= j < tall else (d ^ 1) * tall + i))
    return lax.ppermute(x, ("dp", "tm"), pairs)


def after(x, *others):
    return lax.optimization_barrier((x, others))[0]


def body(latents, cotangent, spatial_weight, temporal_weight):
    clips, frames, rows, cols, chans = latents.shape
    planes, shift = frames * clips, clips * cols
    cells = planes * cols
    lat = jnp.swapaxes(latents, 0, 1).reshape(planes, rows, cols, chans)
    cot = jnp.swapaxes(cotangent, 0, 1).reshape(planes, rows, cols, chans)
    scale = (clips * lax.axis_size("dp") * frames * rows * lax.axis_size("tm") * cols) ** (-0.5)
    groups, ends = groups_of(2 * chans)
    code = codes(groups)
    unit = 2 * cells * chans * chans

    def lat_row(source, place):
        row = lax.axis_index("tm") % 2 * (rows - 1 - 2 * place) + place
        return lax.dynamic_index_in_dim(source, row, 1, keepdims=False).reshape(cells, chans)

    there = {}
    lat_far = from_far(lat_row(lat, 0))
    taps = pltpu.VMEM((3, cells, chans), F32)
    padded = pltpu.VMEM((cells + 2 * shift, chans), BF16)
    (act_grad,) = call(
        functools.partial(act_grad_kernel, shift), [pltpu.HBM((rows, cells, chans), BF16)], [padded], 10,
        3 * rows * unit, [code, cot, temporal_weight],
    )
    lat_near = from_near(lat_row(after(lat, act_grad), rows - 1))
    (pre_loc,) = call(
        pre_kernel, [pltpu.HBM((rows, cells, chans), F32)], [taps], 10, (9 * rows - 6) * unit,
        [code, after(lat, act_grad), spatial_weight],
    )
    narrow = jax.ShapeDtypeStruct((cells, chans), BF16)
    count = rows - 1
    early = call(
        functools.partial(early_kernel, shift),
        [narrow] * (2 * count)
        + [
            pltpu.VMEM((4 * chans, 3 * chans), F32),
            pltpu.VMEM((cells, chans), F32),
            pltpu.VMEM((cells, chans), BF16),
            pltpu.VMEM((planes, cols, 3 * chans), BF16),
            pltpu.VMEM((2, planes, cols, chans), BF16),
        ],
        [
            taps,
            pltpu.VMEM((rows, planes, cols, chans), BF16),
            pltpu.VMEM((count, cells, 3 * chans), BF16),
            pltpu.VMEM((count, planes, cols, 3 * chans), BF16),
            pltpu.VMEM((count, cells, chans), F32),
            pltpu.VMEM((count, cells, chans), BF16),
            pltpu.SemaphoreType.DMA((rows, 6)),
            pltpu.SemaphoreType.DMA((7,)),
        ],
        16, (3 + 12 * count) * unit, [code, lat, cot, keep(lat_far), pre_loc, act_grad, keep(spatial_weight)],
        far=(1, 2, 4, 5),
    )
    acts, pgs = list(early[:count]), list(early[count : 2 * count])
    cut, near_cut = (round(planes * part) * cols for part in (FAR_CUT, NEAR_CUT))
    there["far"] = from_far(after(pgs[0][:cut], lat_near))
    half = pltpu.VMEM((2 * chans, 3 * chans), BF16)
    act, pg, spread, other = call(
        functools.partial(late_kernel, ends, scale),
        [narrow, narrow, pltpu.VMEM((cells, 3 * chans), BF16), half], [taps], 8, 9 * unit,
        [code, *map(keep, (lat_near, spatial_weight, *early[2 * count :]))],
    )
    (mine,) = call(
        functools.partial(own_kernel, ends, scale), [half], [], 8, 6 * unit,
        [code, *map(keep, (lat_near, early[2 * count], *early[2 * count + 3 :], act, spread))],
    )
    acts, pgs = acts + [act], pgs + [pg]
    image = jax.ShapeDtypeStruct(lat.shape, BF16)

    def beside_first(gate):
        (block_out,) = call(
            functools.partial(out_kernel, shift), [image], [padded], 12, 3 * rows * unit,
            [code, lat, *acts, temporal_weight],
        )
        later.append(from_near(after(pgs[-1][:near_cut], gate)))
        later.append(from_far(after(pgs[0][cut:], gate)))
        return {"far": there["far"], "out": block_out}

    def beside_second(_):
        (back_loc,) = call(
            back_kernel, [jax.ShapeDtypeStruct((rows, cells, chans), F32)], [taps], 12,
            (9 * rows - 6) * unit, [code, cot, *pgs, spatial_weight],
        )
        return {"near": later[0], "back": back_loc, "rest": later[1]}

    def beside_fourth(gate):
        return {"last": from_near(after(pgs[-1][near_cut:], gate))}

    def beside_last(_):
        (latents_grad,) = call(
            last_kernel, [image], [taps, pltpu.VMEM((2, cells, chans), BF16)], 12, 6 * unit,
            [code, there["back"], keep(spatial_weight), *(keep(there[name]) for name in ("far", "rest", "near", "last"))],
        )
        return {"grad": latents_grad}

    def ordered(sums, *given):
        return call(
            functools.partial(order_kernel, ends, not given),
            [jax.ShapeDtypeStruct((3, 3, chans, chans), F32), jax.ShapeDtypeStruct((3, chans, chans), F32)],
            [pltpu.VMEM((2, 3, chans, chans), F32), pltpu.SemaphoreType.DMA((2,))],
            8, 0, [code, keep(sums), *given],
            far=(2, 3), out_far=True, aliases={2: 0, 3: 1} if given else None,
        )

    later = []
    beside = [beside_first, beside_second, lambda _: {}, beside_fourth, beside_last]
    mine, other = add_up(mine, other, groups, beside, there)
    block_out, latents_grad = there["out"], there["grad"]
    spatial_grad, temporal_grad = ordered(other, *ordered(mine))

    def home(x):
        return jnp.swapaxes(x.reshape(frames, clips, rows, cols, chans), 0, 1)

    return home(block_out), home(latents_grad), spatial_grad, temporal_grad


def solution(mesh):
    in_specs = (P("dp", None, "tm", None, None), P("dp", None, "tm", None, None), P(), P())
    out_specs = (P("dp", None, "tm", None, None), P("dp", None, "tm", None, None), P(), P())
    return jax.shard_map(body, mesh=mesh, in_specs=in_specs, out_specs=out_specs, check_vma=False)
```
